128 devices in a mesh: inner: 16 (over y, x), outer: 8 (over z, core).
Axes of the slice: x: 4, y: 4, z: 4, core: 2. Of those that a mesh axis runs over, the one named last changes fastest.
Arguments:
- embedding: bfloat16 [393216, 4096], P(('inner', 'outer')), may hold values from -80 to 80
- test_matrix: bfloat16 [4096, 256], replicated, may hold values from -0.09375 to 0.09375
Outputs:
- projection: float32 [4096, 256], P(('inner', 'outer'))
The draws below stay inside these ranges and needn't reach their ends.
All inputs are finite; a program needn't handle non-finite values.
Results may differ from the reference program's by a relative error of at most 0.00035.
Values sent between devices are 32-bit elements; how exact they have to be, the bound alone decides.
No kernel may reach another device: no remote copies, remote signals or barrier semaphores. Data moves between devices by JAX's collectives and lax.ppermute only.
A program may use at most 128 MiB of HBM per device.

```python
import jax
import jax.numpy as jnp
from jax import lax

D = 4096
K = 256
ROWS = 393216


def draw_embedding(key, part):
    key = jax.random.fold_in(key, 11)
    key_base, key_rows, key_cols = jax.random.split(key, 3)
    position = jnp.arange(ROWS, dtype=jnp.float32) / ROWS
    base = jax.random.truncated_normal(key_base, -5.0, 5.0, (ROWS, D), jnp.float32)
    spread = 10.0
    row_scale = jnp.power(3.0, position) * jnp.power(spread, jax.random.uniform(key_rows, (ROWS,), jnp.float32)) / 4.0
    col_scale = jnp.power(spread, jax.random.uniform(key_cols, (D,), jnp.float32)) * 2.0 / spread
    return (base * row_scale[:, None] * col_scale[None, :]).astype(jnp.bfloat16)


def centred(own_key, dims, width, reach, kind=jnp.bfloat16):
    result = jax.random.normal(own_key, dims, jnp.float32) * width
    return jnp.minimum(jnp.maximum(result, -reach), reach).astype(kind)


def setup_inputs(seed: int = 0) -> dict:
    keys = jax.random.split(jax.random.key(seed), 3)
    return {
        "embedding": draw_embedding(jax.random.fold_in(keys[2], 71), 0),
        "test_matrix": centred(keys[1], (D, K), D ** -0.5, 0.09375),
    }


def reference(embedding, test_matrix):
    sketch = jnp.dot(embedding.astype(jnp.float32), test_matrix.astype(jnp.float32), preferred_element_type=jnp.float32)
    gram = jnp.dot(sketch.T.astype(jnp.float32), sketch.astype(jnp.float32), precision=lax.Precision.HIGHEST, preferred_element_type=jnp.float32)
    lower = jnp.linalg.cholesky(gram)
    basis = lax.linalg.triangular_solve(lower, sketch, left_side=False, lower=True, transpose_a=True).astype(jnp.bfloat16)
    return lax.dot_general(embedding.astype(jnp.float32), basis.astype(jnp.float32), (((0,), (0,)), ((), ())), preferred_element_type=jnp.float32)
```

```python
import jax
import jax.numpy as jnp
from jax import lax
from jax.experimental import pallas as pl
from jax.experimental.pallas import tpu as pltpu
from jax.sharding import Mesh, PartitionSpec as P

K = 256
B = 8
MIB = 1 << 20


def tree(terms):
    while len(terms) > 1:
        terms = [
            terms[i] + terms[i + 1] if i + 1 < len(terms) else terms[i]
            for i in range(0, len(terms), 2)
        ]
    return terms[0]


def sketch_kernel(e_ref, t_ref, st_ref, gram_ref, cross_ref):
    i = pl.program_id(0)
    s = jnp.dot(e_ref[...], t_ref[...], preferred_element_type=jnp.float32)
    hi = s.astype(jnp.bfloat16)
    rest = s - hi.astype(jnp.float32)
    mid = rest.astype(jnp.bfloat16)
    lo = (rest - mid.astype(jnp.float32)).astype(jnp.bfloat16)
    st = s.T
    hi_t = st.astype(jnp.bfloat16)
    mid_t = (st - hi_t.astype(jnp.float32)).astype(jnp.bfloat16)
    st_ref[0:K, :] = hi_t
    st_ref[K : 2 * K, :] = mid_t
    f32 = jnp.float32
    square = jnp.dot(hi_t, hi, preferred_element_type=f32) + jnp.dot(
        mid_t, mid, preferred_element_type=f32
    )
    cross = jnp.dot(hi_t, mid, preferred_element_type=f32) + jnp.dot(
        hi_t, lo, preferred_element_type=f32
    )

    @pl.when(i == 0)
    def _():
        gram_ref[...] = square
        cross_ref[...] = cross

    @pl.when(i > 0)
    def _():
        gram_ref[...] += square
        cross_ref[...] += cross

    @pl.when(i == pl.num_programs(0) - 1)
    def _():
        both = cross_ref[...]
        gram_ref[...] += both + both.T


def sketch_and_gram(e, t):
    rows, d = e.shape
    r = 512
    return pl.pallas_call(
        sketch_kernel,
        grid=(rows // r,),
        in_specs=[
            pl.BlockSpec((r, d), lambda i: (i, 0)),
            pl.BlockSpec((d, K), lambda i: (0, 0)),
        ],
        out_specs=[
            pl.BlockSpec((2 * K, r), lambda i: (0, i)),
            pl.BlockSpec((K, K), lambda i: (0, 0)),
        ],
        out_shape=[
            jax.ShapeDtypeStruct((2 * K, rows), jnp.bfloat16),
            jax.ShapeDtypeStruct((K, K), jnp.float32),
        ],
        scratch_shapes=[pltpu.VMEM((K, K), jnp.float32)],
        compiler_params=pltpu.CompilerParams(vmem_limit_bytes=40 * MIB),
        cost_estimate=pl.CostEstimate(
            flops=2 * rows * K * (d + 4 * K),
            bytes_accessed=rows * d * 2 + d * K * 2 + rows * K * 4,
            transcendentals=0,
        ),
        name="sketch",
    )(e, t)


def product_kernel(core_ref, e_ref, st_ref, keep_ref, send_ref):
    mt = jnp.dot(st_ref[...], e_ref[...], preferred_element_type=jnp.float32)
    m = (mt[0:K] + mt[K : 2 * K]).T
    m = m.reshape(keep_ref.shape[0], 2, 32, K)
    core = core_ref[0]

    @pl.when(core == 0)
    def _():
        keep_ref[...] = m[:, 0]
        send_ref[...] = m[:, 1]

    @pl.when(core != 0)
    def _():
        keep_ref[...] = m[:, 1]
        send_ref[...] = m[:, 0]


def product(core, e, st):
    rows, d = e.shape
    cols = 512
    n = cols // 64
    half = jax.ShapeDtypeStruct((d // 64, 32, K), jnp.float32)
    spec = pl.BlockSpec((n, 32, K), lambda i: (i, 0, 0))
    return pl.pallas_call(
        product_kernel,
        grid=(d // cols,),
        in_specs=[
            pl.BlockSpec(memory_space=pltpu.SMEM),
            pl.BlockSpec((rows, cols), lambda i: (0, i)),
            pl.BlockSpec((2 * K, rows), lambda i: (0, 0)),
        ],
        out_specs=[spec, spec],
        out_shape=[half, half],
        compiler_params=pltpu.CompilerParams(vmem_limit_bytes=40 * MIB),
        cost_estimate=pl.CostEstimate(
            flops=4 * rows * K * d,
            bytes_accessed=rows * d * 2 + rows * K * 4 + d * K * 4,
            transcendentals=0,
        ),
        name="product",
    )(core, e, st)


def small_inverse(d):
    n = len(d)
    d = [list(row) for row in d]
    l = [[None] * n for _ in range(n)]
    w = [[None] * n for _ in range(n)]
    for i in range(n):
        inv = lax.rsqrt(d[i][i])
        w[i][i] = inv
        for a in range(i + 1, n):
            l[a][i] = d[a][i] * inv
        for a in range(i + 1, n):
            for b in range(i + 1, a + 1):
                d[a][b] = d[a][b] - l[a][i] * l[b][i]
        for b in range(i):
            w[i][b] = -inv * tree([l[i][k] * w[k][b] for k in range(b, i)])
    return w


def inverse_factor_kernel(g_ref, x):
    x[...] = g_ref[...]
    lane = lax.broadcasted_iota(jnp.int32, (B, 128), 1)
    for j in range(K // B):
        b0 = j * B
        h, o = divmod(b0, 128)
        inside = (lane >= o) & (lane < o + B)
        panel = x[b0 : b0 + B, h * 128 : (h + 1) * 128]
        cols = [jnp.broadcast_to(panel[:, o + b : o + b + 1], (B, 128)) for b in range(B)]
        d = [
            [jnp.broadcast_to(cols[b][a : a + 1, :], (B, 128)) for b in range(a + 1)]
            for a in range(B)
        ]
        w = small_inverse(d)
        dinv = [[None] * B for _ in range(B)]
        for a in range(B):
            for b in range(a + 1):
                v = tree([w[k][a] * w[k][b] for k in range(a, B)])
                dinv[a][b] = dinv[b][a] = v
        rows = []
        for half in range(2):
            part = []
            for a in range(B):
                r = jnp.broadcast_to(
                    x[b0 + a : b0 + a + 1, half * 128 : (half + 1) * 128], (B, 128)
                )
                if half == h:
                    r = jnp.where(inside, jnp.where(lane == o + a, 1.0, 0.0), r)
                part.append(r)
            rows.append(part)
        y = [
            [tree([dinv[k][a] * rows[half][a] for a in range(B)]) for k in range(B)]
            for half in range(2)
        ]
        for r in range(j + 1, K // B):
            sl = slice(r * B, (r + 1) * B)
            old = [x[sl, 0:128], x[sl, 128:256]]
            c = [
                jnp.broadcast_to(old[h][:, o + k : o + k + 1], (B, 128)) for k in range(B)
            ]
            for half in range(2):
                base = old[half]
                if half == h:
                    base = jnp.where(inside, 0.0, base)
                x[sl, half * 128 : (half + 1) * 128] = base - tree(
                    [c[k] * y[half][k] for k in range(B)]
                )
        for half in range(2):
            for i in range(B):
                if half > h:
                    v = jnp.zeros((1, 128), jnp.float32)
                else:
                    v = tree([w[i][k] * rows[half][k] for k in range(i + 1)])
                    if half == h:
                        v = jnp.where(lane < o + B, v, 0.0)
                x[b0 + i : b0 + i + 1, half * 128 : (half + 1) * 128] = v[0:1, :]


def inverse_factor(g):
    return pl.pallas_call(
        inverse_factor_kernel,
        out_shape=jax.ShapeDtypeStruct((K, K), jnp.float32),
        in_specs=[pl.BlockSpec(memory_space=pltpu.VMEM)],
        out_specs=pl.BlockSpec(memory_space=pltpu.VMEM),
        compiler_params=pltpu.CompilerParams(vmem_limit_bytes=32 * MIB),
        cost_estimate=pl.CostEstimate(
            flops=12_000_000_000, bytes_accessed=1 << 19, transcendentals=256
        ),
        name="inverse_factor",
    )(g)


def finish_kernel(parts_ref, w_ref, out_ref):
    m = jnp.sum(parts_ref[...], axis=0)
    out_ref[...] = lax.dot_general(
        m,
        w_ref[...],
        (((1,), (1,)), ((), ())),
        precision=lax.Precision.HIGHEST,
        preferred_element_type=jnp.float32,
    )


def finish(parts, w):
    return pl.pallas_call(
        finish_kernel,
        out_shape=jax.ShapeDtypeStruct((32, K), jnp.float32),
        in_specs=[pl.BlockSpec(memory_space=pltpu.VMEM)] * 2,
        out_specs=pl.BlockSpec(memory_space=pltpu.VMEM),
        compiler_params=pltpu.CompilerParams(vmem_limit_bytes=32 * MIB),
        name="finish",
    )(parts, w)


def solution(mesh):
    chips = ("y", "x", "z")
    every = chips + ("core",)
    fine = Mesh(mesh.devices.reshape(4, 4, 4, 2), every)
    swap = [(0, 1), (1, 0)]

    def local(embedding, test_matrix):
        core = lax.axis_index("core").astype(jnp.int32).reshape(1)
        st, gram = sketch_and_gram(embedding, test_matrix)
        pieces = lax.all_to_all(gram.reshape(128, 2, K), every, 0, 0, tiled=True)
        keep, send = product(core, embedding, st)
        mine = keep + lax.ppermute(send, "core", swap)
        parts = lax.all_to_all(mine, chips, 0, 0, tiled=True)
        rows = jnp.sum(pieces, axis=0)
        gram = lax.all_to_all(
            jnp.broadcast_to(rows, (128, 2, K)), every, 0, 0, tiled=True
        ).reshape(K, K)
        return finish(parts, inverse_factor(gram))

    return jax.shard_map(
        local,
        mesh=fine,
        in_specs=(P(every, None), P()),
        out_specs=P(every, None),
        check_vma=False,
    )
```

```python
import functools

import jax
import jax.numpy as jnp
from jax import lax
from jax.experimental import pallas as pl
from jax.experimental.pallas import tpu as pltpu
from jax.sharding import Mesh, PartitionSpec as P

K = 256
B = 8
HALF = K // 2
MIB = 1 << 20


def tree(terms):
    while len(terms) > 1:
        terms = [
            terms[i] + terms[i + 1] if i + 1 < len(terms) else terms[i]
            for i in range(0, len(terms), 2)
        ]
    return terms[0]


ROWS_STEP = 512
COLS_STEP = 1024
CHIPS_STEP = COLS_STEP // 64
PACKED = 3
OVER_ROWS = (((0,), (0,)), ((), ()))


def local_kernel(
    steps, place_ref, e_ref, t_ref, keep_0, keep_1, send_0, send_1, gram_keep_ref,
    gram_send_ref, held, s_ref, gram, parts, sem,
):
    i = pl.program_id(0)
    f32 = jnp.float32
    x, z, core = place_ref[1], place_ref[2], place_ref[3]
    last = steps - 1
    short = ROWS_STEP // 2

    def span(step, rows):
        start = jnp.where(step == 0, 0, step * ROWS_STEP - short)
        return pl.ds(pl.multiple_of(start, short), rows)

    def fetch(step, rows):
        r = span(step, rows)
        return pltpu.make_async_copy(e_ref.at[r], held.at[r], sem.at[step])

    def sketch(rows):
        fetch(i, rows).wait()

        @pl.when(i + 2 < last)
        def _():
            fetch(i + 2, ROWS_STEP).start()

        @pl.when(i + 2 == last)
        def _():
            fetch(i + 2, short).start()

        r = span(i, rows)
        s = jnp.dot(held[r, :], t_ref[...], preferred_element_type=f32)
        hi = s.astype(jnp.bfloat16)
        s_ref[r, 0:K] = hi
        s_ref[r, K : 2 * K] = (s - hi.astype(f32)).astype(jnp.bfloat16)

    @pl.when(i == 0)
    def _():
        fetch(0, short).start()
        fetch(1, ROWS_STEP).start()

    @pl.when((i == 0) | (i == last))
    def _():
        sketch(short)

    @pl.when((i > 0) & (i < last))
    def _():
        sketch(ROWS_STEP)

    @pl.when(i == steps)
    def _():
        g = lax.dot_general(s_ref[...], s_ref[...], OVER_ROWS, preferred_element_type=f32)
        gram[...] = (g[0:K, 0:K] + g[K:, K:]) + (g[0:K, K:] + g[K:, 0:K])

        def pack(out, c):
            diagonal = gram[c * HALF : (c + 1) * HALF, c * HALF : (c + 1) * HALF]
            below = gram[HALF + 64 * c : HALF + 64 * (c + 1), 0:HALF]
            out[:, :, 0:HALF] = diagonal[0:96].reshape(PACKED, 32, HALF)
            out[0, :, HALF:K] = diagonal[96:128]
            out[1:3, :, HALF:K] = below.reshape(2, 32, HALF)

        @pl.when(core == 0)
        def _():
            pack(gram_keep_ref, 0)
            pack(gram_send_ref, 1)

        @pl.when(core != 0)
        def _():
            pack(gram_keep_ref, 1)
            pack(gram_send_ref, 0)

    @pl.when(i >= steps)
    def _():
        c = pl.ds(pl.multiple_of((i - steps) * COLS_STEP, COLS_STEP), COLS_STEP)
        m = lax.dot_general(held[:, c], s_ref[...], OVER_ROWS, preferred_element_type=f32)
        parts[...] = (m[:, 0:K] + m[:, K : 2 * K]).reshape(CHIPS_STEP, 2, 32, K)
        for f, (keep_ref, send_ref) in enumerate(((keep_0, send_0), (keep_1, send_1))):
            for n in range(4):
                for g in range(2):
                    by_zero = 4 * flip(flip(x, f), 2 * g) + ((z + n) & 3)
                    by_one = 4 * flip(flip(x, 2 * f), g) + n
                    zero = core == 0
                    keep_ref[0, n, g] = parts[jnp.where(zero, by_zero, by_one), core]
                    send_ref[0, n, g] = parts[jnp.where(zero, by_one, by_zero), 1 - core]


def blocks(*lead):
    return jax.ShapeDtypeStruct(lead + (32, K), jnp.float32)


def local_products(place, e, t):
    rows, d = e.shape
    steps = rows // ROWS_STEP + 1

    def column(i):
        return jnp.maximum(i - steps, 0)

    def mine(i, p):
        return (jnp.where(p[3] == 0, column(i), (column(i) - p[0]) & 3), 0, 0, 0, 0)

    def theirs(i, p):
        return (jnp.where(p[3] != 0, column(i), (column(i) - p[0]) & 3), 0, 0, 0, 0)

    block = (1, 4, 2, 32, K)
    whole = pl.BlockSpec((PACKED, 32, K), lambda i, p: (0, 0, 0))
    return pl.pallas_call(
        functools.partial(local_kernel, steps),
        grid_spec=pltpu.PrefetchScalarGridSpec(
            num_scalar_prefetch=1,
            grid=(steps + d // COLS_STEP,),
            in_specs=[
                pl.BlockSpec(memory_space=pl.ANY),
                pl.BlockSpec((d, K), lambda i, p: (0, 0)),
            ],
            out_specs=[pl.BlockSpec(block, mine)] * 2
            + [pl.BlockSpec(block, theirs)] * 2
            + [whole] * 2,
            scratch_shapes=[
                pltpu.VMEM((rows, d), jnp.bfloat16),
                pltpu.VMEM((rows, 2 * K), jnp.bfloat16),
                pltpu.VMEM((K, K), jnp.float32),
                pltpu.VMEM((CHIPS_STEP, 2, 32, K), jnp.float32),
                pltpu.SemaphoreType.DMA((steps,)),
            ],
        ),
        out_shape=[blocks(4, 4, 2)] * 4 + [blocks(PACKED)] * 2,
        compiler_params=pltpu.CompilerParams(vmem_limit_bytes=46 * MIB),
        cost_estimate=pl.CostEstimate(
            flops=6 * rows * K * d + 8 * rows * K * K,
            bytes_accessed=rows * d * 2 + d * K * 6,
            transcendentals=0,
        ),
        name="local_products",
    )(place, e, t)


def one_step(kernel, name, out_shape):
    vmem = pl.BlockSpec(memory_space=pltpu.VMEM)

    def call(*args, scratch=()):
        return pl.pallas_call(
            kernel,
            out_shape=out_shape,
            in_specs=[vmem] * len(args),
            out_specs=[vmem] * len(out_shape),
            scratch_shapes=list(scratch),
            compiler_params=pltpu.CompilerParams(vmem_limit_bytes=20 * MIB),
            name=name,
        )(*args)

    return call


def piece_at(core, d, o):
    return jnp.where(core == 0, o, d), jnp.where(core == 0, d, o)


def message_kernel(d, keep_ref, got_ref, gk_ref, gg_ref, out_ref):
    for o in range(4):
        a, n = piece_at(lax.axis_index("core"), d, o)
        out_ref[2 * o : 2 * o + 2] = keep_ref[a, n] + got_ref[a, n]
    out_ref[8:] = gk_ref[...] + gg_ref[...]


def message(d, keep, got, gk, gg):
    kernel = functools.partial(message_kernel, d)
    return one_step(kernel, "message", [blocks(8 + PACKED)])(keep, got, gk, gg)[0]


def second_kernel(keep_ref, got_ref, gk_ref, gg_ref, *refs):
    arrived, own, out, m = refs[:7], refs[7], refs[8:15], refs[15]
    core = lax.axis_index("core")
    for o in range(4):
        a, n = piece_at(core, 0, o)
        m[o] = (keep_ref[a, n] + got_ref[a, n]) + tree(
            [r[2 * o : 2 * o + 2] for r in arrived]
        )
    gram = (gk_ref[...] + gg_ref[...]) + tree([r[8:] for r in arrived])
    at = jnp.where(core == 0, lax.axis_index("y"), lax.axis_index("z"))
    own[...] = m[at, 0]
    for ref, (e, g) in zip(out, MOVES):
        ref[0] = m[(at + e) & 3, g]
        ref[1:] = gram


def second(keep, got, gk, gg, arrived):
    outs = [blocks()] + [blocks(1 + PACKED)] * 7
    scratch = [pltpu.VMEM((4, 2, 32, K), jnp.float32)]
    return one_step(second_kernel, "second", outs)(
        keep, got, gk, gg, *arrived, scratch=scratch
    )


def last_kernel(own_ref, sent_ref, *refs):
    arrived, m_ref, g_ref = refs[:7], refs[7], refs[8]
    m_ref[...] = own_ref[...] + tree([r[0] for r in arrived])
    g_ref[...] = sent_ref[1:] + tree([r[1:] for r in arrived])


def last(own, sent, arrived):
    return one_step(last_kernel, "last", [blocks(), blocks(PACKED)])(own, sent, *arrived)


def small_inverse(d):
    n = len(d)
    d = [list(row) for row in d]
    l = [[None] * n for _ in range(n)]
    w = [[None] * n for _ in range(n)]
    for i in range(n):
        inv = lax.rsqrt(d[i][i])
        w[i][i] = inv
        for a in range(i + 1, n):
            l[a][i] = d[a][i] * inv
        for a in range(i + 1, n):
            for b in range(i + 1, a + 1):
                d[a][b] = d[a][b] - l[a][i] * l[b][i]
        for b in range(i):
            w[i][b] = -inv * tree([l[i][k] * w[k][b] for k in range(b, i)])
    return w


def chol_inverse(x):
    lane = lax.broadcasted_iota(jnp.int32, (B, HALF), 1)
    n = HALF // B

    def spread(j):
        o = j * B
        panel = x[o : o + B, :]
        cols = [
            jnp.broadcast_to(panel[:, o + b : o + b + 1], (B, HALF)) for b in range(B)
        ]
        return [
            [jnp.broadcast_to(cols[b][a : a + 1, :], (B, HALF)) for b in range(a + 1)]
            for a in range(B)
        ]

    w = small_inverse(spread(0))
    for j in range(n):
        o = j * B
        inside = (lane >= o) & (lane < o + B)
        rows = []
        for a in range(B):
            r = jnp.broadcast_to(x[o + a : o + a + 1, :], (B, HALF))
            rows.append(jnp.where(inside, jnp.where(lane == o + a, 1.0, 0.0), r))
        v = [tree([w[i][k] * rows[k] for k in range(i + 1)]) for i in range(B)]
        if j + 1 < n:
            y = [tree([w[i][k] * v[i] for i in range(k, B)]) for k in range(B)]
        for r in range(j + 1, n):
            sl = slice(r * B, (r + 1) * B)
            old = x[sl, :]
            c = [jnp.broadcast_to(old[:, o + k : o + k + 1], (B, HALF)) for k in range(B)]
            x[sl, :] = jnp.where(inside, 0.0, old) - tree([c[k] * y[k] for k in range(B)])
            if r == j + 1:
                w = small_inverse(spread(r))
        for i in range(B):
            x[o + i : o + i + 1, :] = jnp.where(lane < o + B, v[i], 0.0)[0:1, :]


def times_transposed(a, b):
    return lax.dot_general(
        a,
        b,
        (((1,), (1,)), ((), ())),
        precision=lax.Precision.HIGHEST,
        preferred_element_type=jnp.float32,
    )


def finish_kernel(m_ref, own_ref, other_ref, out_ref, a, b):
    core = lax.axis_index("core")
    zero = jnp.where(core == 0, own_ref[...], other_ref[...])
    one = jnp.where(core == 0, other_ref[...], own_ref[...])

    def unpack(packed):
        left = packed[:, :, 0:HALF].reshape(96, HALF)
        right = packed[:, :, HALF:K].reshape(96, HALF)
        return jnp.concatenate([left, right[0:32]], axis=0), right[32:96]

    a[...], upper = unpack(zero)
    corner, lower = unpack(one)
    below = jnp.concatenate([upper, lower], axis=0)
    chol_inverse(a)
    factor = times_transposed(below, a[...])
    b[...] = corner - times_transposed(factor, factor)
    first = times_transposed(m_ref[:, 0:HALF], a[...])
    rest = m_ref[:, HALF:K] - times_transposed(first, factor)
    chol_inverse(b)
    out_ref[:, 0:HALF] = first
    out_ref[:, HALF:K] = times_transposed(rest, b[...])


def finish(m, own, other):
    vmem = pl.BlockSpec(memory_space=pltpu.VMEM)
    return pl.pallas_call(
        finish_kernel,
        out_shape=blocks(),
        in_specs=[vmem] * 3,
        out_specs=vmem,
        scratch_shapes=[pltpu.VMEM((HALF, HALF), jnp.float32)] * 2,
        compiler_params=pltpu.CompilerParams(vmem_limit_bytes=32 * MIB),
        name="finish",
    )(m, own, other)


MOVES = [(2, 1), (1, 1), (3, 1), (0, 1), (2, 0), (1, 0), (3, 0)]


def flip(x, how):
    return x ^ (0, 1, 3)[how]


def step_pairs(step, move):
    d, f = move
    pairs = []
    for source in range(128):
        y, x, z, core = source // 32, source // 8 % 4, source // 2 % 4, source % 2
        if core == step:
            z = (z + d) % 4
            x = flip(x, f)
        else:
            y = (y + d) % 4
            x = flip(x, 2 * f)
        pairs.append((source, ((y * 4 + x) * 4 + z) * 2 + core))
    return pairs


def solution(mesh):
    every = ("y", "x", "z", "core")
    fine = Mesh(mesh.devices.reshape(4, 4, 4, 2), every)
    swap = [(0, 1), (1, 0)]

    def send_all(step, messages):
        return [
            lax.ppermute(m, every, step_pairs(step, move))
            for m, move in zip(messages, MOVES)
        ]

    def local(embedding, test_matrix):
        place = jnp.stack([lax.axis_index(a) for a in every]).astype(jnp.int32)
        *halves, gk, gs = local_products(place, embedding, test_matrix)
        keep, send = halves[:2], halves[2:]
        gg = lax.ppermute(gs, "core", swap)
        later, gg = lax.optimization_barrier((send[0], gg))
        got = [lax.ppermute(s, "core", swap) for s in (later, send[1])]
        messages = [message(d, keep[f], got[f], gk, gg) for d, f in MOVES]
        arrived = send_all(0, messages)
        own, *messages = second(keep[0], got[0], gk, gg, arrived)
        arrived = send_all(1, messages)
        m, g = last(own, messages[0], arrived)
        return finish(m, g, lax.ppermute(g, "core", swap))

    return jax.shard_map(
        local,
        mesh=fine,
        in_specs=(P(every, None), P()),
        out_specs=P(every, None),
        check_vma=False,
    )
```

```python
import functools

import jax
import jax.numpy as jnp
from jax import lax
from jax.experimental import pallas as pl
from jax.experimental.pallas import tpu as pltpu
from jax.sharding import Mesh, PartitionSpec as P

K = 256
B = 8
HALF = K // 2
MIB = 1 << 20


def tree(terms):
    while len(terms) > 1:
        terms = [
            terms[i] + terms[i + 1] if i + 1 < len(terms) else terms[i]
            for i in range(0, len(terms), 2)
        ]
    return terms[0]


ROWS_STEP = 768
COLS_STEP = 1024
CHIPS_STEP = COLS_STEP // 64
PACKED = 3
OVER_ROWS = (((0,), (0,)), ((), ()))


def local_kernel(
    steps, place_ref, e_ref, t_ref, keep_0, keep_1, send_0, send_1, gram_keep_ref,
    gram_send_ref, held, t_held, s_ref, gram, parts, sem, t_sem,
):
    i = pl.program_id(0)
    f32 = jnp.float32
    x, z, core = place_ref[1], place_ref[2], place_ref[3]

    def fetch(step):
        r = pl.ds(pl.multiple_of(step * ROWS_STEP, ROWS_STEP), ROWS_STEP)
        return pltpu.make_async_copy(e_ref.at[r], held.at[r], sem.at[step])

    @pl.when(i == 0)
    def _():
        table = pltpu.make_async_copy(t_ref, t_held, t_sem)
        table.start()
        fetch(0).start()
        table.wait()
        fetch(1).start()

    @pl.when(i < steps)
    def _():
        fetch(i).wait()

        @pl.when(i + 2 < steps)
        def _():
            fetch(i + 2).start()

        r = pl.ds(pl.multiple_of(i * ROWS_STEP, ROWS_STEP), ROWS_STEP)
        s = jnp.dot(held[r, :], t_held[...], preferred_element_type=f32)
        hi = s.astype(jnp.bfloat16)
        s_ref[r, 0:K] = hi
        s_ref[r, K : 2 * K] = (s - hi.astype(f32)).astype(jnp.bfloat16)

    @pl.when(i == steps)
    def _():
        g = lax.dot_general(
            s_ref[:, 0:K], s_ref[...], OVER_ROWS, preferred_element_type=f32
        )
        mixed = g[:, K : 2 * K]
        gram[...] = g[:, 0:K] + (mixed + mixed.T)

        def pack(out, c):
            diagonal = gram[c * HALF : (c + 1) * HALF, c * HALF : (c + 1) * HALF]
            below = gram[HALF + 64 * c : HALF + 64 * (c + 1), 0:HALF]
            out[:, :, 0:HALF] = diagonal[0:96].reshape(PACKED, 32, HALF)
            out[0, :, HALF:K] = diagonal[96:128]
            out[1:3, :, HALF:K] = below.reshape(2, 32, HALF)

        @pl.when(core == 0)
        def _():
            pack(gram_keep_ref, 0)
            pack(gram_send_ref, 1)

        @pl.when(core != 0)
        def _():
            pack(gram_keep_ref, 1)
            pack(gram_send_ref, 0)

    @pl.when(i >= steps)
    def _():
        c = pl.ds(pl.multiple_of((i - steps) * COLS_STEP, COLS_STEP), COLS_STEP)
        m = lax.dot_general(held[:, c], s_ref[...], OVER_ROWS, preferred_element_type=f32)
        parts[...] = (m[:, 0:K] + m[:, K : 2 * K]).reshape(CHIPS_STEP, 2, 32, K)
        for f, (keep_ref, send_ref) in enumerate(((keep_0, send_0), (keep_1, send_1))):
            for n in range(4):
                for g in range(2):
                    by_zero = 4 * flip(flip(x, f), 2 * g) + ((z + n) & 3)
                    by_one = 4 * flip(flip(x, 2 * f), g) + n
                    zero = core == 0
                    keep_ref[0, n, g] = parts[jnp.where(zero, by_zero, by_one), core]
                    send_ref[0, n, g] = parts[jnp.where(zero, by_one, by_zero), 1 - core]


def blocks(*lead):
    return jax.ShapeDtypeStruct(lead + (32, K), jnp.float32)


def local_products(place, e, t):
    rows, d = e.shape
    steps = rows // ROWS_STEP

    def column(i):
        return jnp.maximum(i - steps, 0)

    def mine(i, p):
        return (jnp.where(p[3] == 0, column(i), (column(i) - p[0]) & 3), 0, 0, 0, 0)

    def theirs(i, p):
        return (jnp.where(p[3] != 0, column(i), (column(i) - p[0]) & 3), 0, 0, 0, 0)

    block = (1, 4, 2, 32, K)
    whole = pl.BlockSpec((PACKED, 32, K), lambda i, p: (0, 0, 0))
    return pl.pallas_call(
        functools.partial(local_kernel, steps),
        grid_spec=pltpu.PrefetchScalarGridSpec(
            num_scalar_prefetch=1,
            grid=(steps + d // COLS_STEP,),
            in_specs=[
                pl.BlockSpec(memory_space=pl.ANY),
                pl.BlockSpec(memory_space=pl.ANY),
            ],
            out_specs=[pl.BlockSpec(block, mine)] * 2
            + [pl.BlockSpec(block, theirs)] * 2
            + [whole] * 2,
            scratch_shapes=[
                pltpu.VMEM((rows, d), jnp.bfloat16),
                pltpu.VMEM((d, K), jnp.bfloat16),
                pltpu.VMEM((rows, 2 * K), jnp.bfloat16),
                pltpu.VMEM((K, K), jnp.float32),
                pltpu.VMEM((CHIPS_STEP, 2, 32, K), jnp.float32),
                pltpu.SemaphoreType.DMA((steps,)),
                pltpu.SemaphoreType.DMA,
            ],
        ),
        out_shape=[blocks(4, 4, 2)] * 4 + [blocks(PACKED)] * 2,
        compiler_params=pltpu.CompilerParams(vmem_limit_bytes=46 * MIB),
        cost_estimate=pl.CostEstimate(
            flops=6 * rows * K * d + 8 * rows * K * K,
            bytes_accessed=rows * d * 2 + d * K * 6,
            transcendentals=0,
        ),
        name="local_products",
    )(place, e, pltpu.with_memory_space_constraint(t, pltpu.HBM))


def one_step(kernel, name, out_shape):
    vmem = pl.BlockSpec(memory_space=pltpu.VMEM)

    def call(*args, scratch=()):
        return pl.pallas_call(
            kernel,
            out_shape=out_shape,
            in_specs=[vmem] * len(args),
            out_specs=[vmem] * len(out_shape),
            scratch_shapes=list(scratch),
            compiler_params=pltpu.CompilerParams(vmem_limit_bytes=20 * MIB),
            name=name,
        )(*args)

    return call


def piece_at(core, d, o):
    return jnp.where(core == 0, o, d), jnp.where(core == 0, d, o)


def message_kernel(d, keep_ref, got_ref, gk_ref, gg_ref, out_ref):
    for o in range(4):
        a, n = piece_at(lax.axis_index("core"), d, o)
        out_ref[2 * o : 2 * o + 2] = keep_ref[a, n] + got_ref[a, n]
    out_ref[8:] = gk_ref[...] + gg_ref[...]


def message(d, keep, got, gk, gg):
    kernel = functools.partial(message_kernel, d)
    return one_step(kernel, "message", [blocks(8 + PACKED)])(keep, got, gk, gg)[0]


def second_kernel(keep_ref, got_ref, gk_ref, gg_ref, *refs):
    arrived, own, out = refs[:7], refs[7], refs[8]
    for o in range(4):
        a, n = piece_at(lax.axis_index("core"), 0, o)
        m = (keep_ref[a, n] + got_ref[a, n]) + tree(
            [r[2 * o : 2 * o + 2] for r in arrived]
        )
        own[o] = m[0]
        out[o] = m[1]
    out[4:] = (gk_ref[...] + gg_ref[...]) + tree([r[8:] for r in arrived])


def second(keep, got, gk, gg, arrived):
    outs = [blocks(4), blocks(4 + PACKED)]
    return one_step(second_kernel, "second", outs)(keep, got, gk, gg, *arrived)


def third_kernel(own_ref, sent, got, own, *refs):
    out, m = refs[:-1], refs[-1]
    m[...] = own_ref[...] + got[0:4]
    gram = sent[4:] + got[4:]
    at = jnp.where(lax.axis_index("core") == 0, lax.axis_index("y"), lax.axis_index("z"))
    own[...] = m[at]
    for ref, d in zip(out, DISTANCES):
        ref[0] = m[(at + d) & 3]
        ref[1:] = gram


def third(own, sent, got):
    outs = [blocks()] + [blocks(1 + PACKED)] * 3
    scratch = [pltpu.VMEM((4, 32, K), jnp.float32)]
    return one_step(third_kernel, "third", outs)(own, sent, got, scratch=scratch)


def last_kernel(own_ref, sent, a, b, c, m_ref, g_ref):
    m_ref[...] = own_ref[...] + (a[0] + b[0] + c[0])
    g_ref[...] = sent[1:] + (a[1:] + b[1:] + c[1:])


def last(own, sent, arrived):
    return one_step(last_kernel, "last", [blocks(), blocks(PACKED)])(own, sent, *arrived)


def small_inverse(d):
    n = len(d)
    d = [list(row) for row in d]
    l = [[None] * n for _ in range(n)]
    w = [[None] * n for _ in range(n)]
    for i in range(n):
        inv = lax.rsqrt(d[i][i])
        w[i][i] = inv
        for a in range(i + 1, n):
            l[a][i] = d[a][i] * inv
        for a in range(i + 1, n):
            for b in range(i + 1, a + 1):
                d[a][b] = d[a][b] - l[a][i] * l[b][i]
        for b in range(i):
            w[i][b] = -inv * tree([l[i][k] * w[k][b] for k in range(b, i)])
    return w


def across(v, lane):
    return jnp.take_along_axis(v, jnp.full(v.shape, lane, jnp.int32), axis=1)


def chol_inverse(x):
    lane = lax.broadcasted_iota(jnp.int32, (B, HALF), 1)
    n = HALF // B

    def spread(j):
        o = j * B
        panel = x[o : o + B, :]
        cols = [across(panel, o + b) for b in range(B)]
        return [
            [jnp.broadcast_to(cols[b][a : a + 1, :], (B, HALF)) for b in range(a + 1)]
            for a in range(B)
        ]

    w = small_inverse(spread(0))
    for j in range(n):
        o = j * B
        inside = (lane >= o) & (lane < o + B)
        rows = []
        for a in range(B):
            r = jnp.broadcast_to(x[o + a : o + a + 1, :], (B, HALF))
            rows.append(jnp.where(inside, jnp.where(lane == o + a, 1.0, 0.0), r))
        v = [tree([w[i][k] * rows[k] for k in range(i + 1)]) for i in range(B)]
        if j + 1 < n:
            y = [tree([w[i][k] * v[i] for i in range(k, B)]) for k in range(B)]
        for r in range(j + 1, n):
            sl = slice(r * B, (r + 1) * B)
            old = x[sl, :]
            c = [across(old, o + k) for k in range(B)]
            x[sl, :] = jnp.where(inside, 0.0, old) - tree([c[k] * y[k] for k in range(B)])
            if r == j + 1:
                w = small_inverse(spread(r))
        for i in range(B):
            x[o + i : o + i + 1, :] = jnp.where(lane < o + B, v[i], 0.0)[0:1, :]


def times_transposed(a, b):
    return lax.dot_general(
        a,
        b,
        (((1,), (1,)), ((), ())),
        precision=lax.Precision.HIGHEST,
        preferred_element_type=jnp.float32,
    )


def finish_kernel(m_ref, own_ref, other_ref, out_ref, a, b):
    core = lax.axis_index("core")
    zero = jnp.where(core == 0, own_ref[...], other_ref[...])
    one = jnp.where(core == 0, other_ref[...], own_ref[...])

    def unpack(packed):
        left = packed[:, :, 0:HALF].reshape(96, HALF)
        right = packed[:, :, HALF:K].reshape(96, HALF)
        return jnp.concatenate([left, right[0:32]], axis=0), right[32:96]

    a[...], upper = unpack(zero)
    corner, lower = unpack(one)
    below = jnp.concatenate([upper, lower], axis=0)
    chol_inverse(a)
    factor = times_transposed(below, a[...])
    b[...] = corner - times_transposed(factor, factor)
    first = times_transposed(m_ref[:, 0:HALF], a[...])
    rest = m_ref[:, HALF:K] - times_transposed(first, factor)
    chol_inverse(b)
    out_ref[:, 0:HALF] = first
    out_ref[:, HALF:K] = times_transposed(rest, b[...])


def finish(m, own, other):
    vmem = pl.BlockSpec(memory_space=pltpu.VMEM)
    return pl.pallas_call(
        finish_kernel,
        out_shape=blocks(),
        in_specs=[vmem] * 3,
        out_specs=vmem,
        scratch_shapes=[pltpu.VMEM((HALF, HALF), jnp.float32)] * 2,
        compiler_params=pltpu.CompilerParams(vmem_limit_bytes=32 * MIB),
        name="finish",
    )(m, own, other)


MOVES = [(2, 1), (1, 1), (3, 1), (0, 1), (2, 0), (1, 0), (3, 0)]
DISTANCES = (2, 1, 3)


def flip(x, how):
    return x ^ (0, 1, 3)[how]


def step_pairs(step, move):
    d, f = move
    pairs = []
    for source in range(128):
        y, x, z, core = source // 32, source // 8 % 4, source // 2 % 4, source % 2
        if core == step:
            z = (z + d) % 4
            x = flip(x, f)
        else:
            y = (y + d) % 4
            x = flip(x, 2 * f)
        pairs.append((source, ((y * 4 + x) * 4 + z) * 2 + core))
    return pairs


def solution(mesh):
    every = ("y", "x", "z", "core")
    fine = Mesh(mesh.devices.reshape(4, 4, 4, 2), every)
    swap = [(0, 1), (1, 0)]

    def send(step, message, move):
        return lax.ppermute(message, every, step_pairs(step, move))

    def local(embedding, test_matrix):
        place = jnp.stack([lax.axis_index(a) for a in every]).astype(jnp.int32)
        *halves, gk, gs = local_products(place, embedding, test_matrix)
        keep, other = halves[:2], halves[2:]
        gg = lax.ppermute(gs, "core", swap)
        later, gg = lax.optimization_barrier((other[0], gg))
        got = [lax.ppermute(s, "core", swap) for s in (later, other[1])]
        messages = [message(d, keep[f], got[f], gk, gg) for d, f in MOVES]
        arrived = [send(0, m, move) for m, move in zip(messages, MOVES)]
        own, message_2 = second(keep[0], got[0], gk, gg, arrived)
        arrived = send(1, message_2, (0, 1))
        own, *messages = third(own, message_2, arrived)
        arrived = [send(1, m, (d, 0)) for m, d in zip(messages, DISTANCES)]
        m, g = last(own, messages[0], arrived)
        return finish(m, g, lax.ppermute(g, "core", swap))

    return jax.shard_map(
        local,
        mesh=fine,
        in_specs=(P(every, None), P()),
        out_specs=P(every, None),
        check_vma=False,
    )
```

```python
import functools

import jax
import jax.numpy as jnp
from jax import lax
from jax.experimental import pallas as pl
from jax.experimental.pallas import tpu as pltpu
from jax.sharding import Mesh, PartitionSpec as P

K = 256
B = 8
HALF = K // 2
MIB = 1 << 20


def tree(terms):
    while len(terms) > 1:
        terms = [
            terms[i] + terms[i + 1] if i + 1 < len(terms) else terms[i]
            for i in range(0, len(terms), 2)
        ]
    return terms[0]


ROWS_STEP = 768
COLS_STEP = 1024
CHIPS_STEP = COLS_STEP // 64
PACKED = 3
OVER_ROWS = (((0,), (0,)), ((), ()))


def local_kernel(
    steps, place_ref, e_ref, t_ref, keep_ref, s0, s1, s2, s3, gram_keep_ref,
    gram_send_ref, held, t_held, s_ref, gram, parts, sem, t_sem,
):
    i = pl.program_id(0)
    f32 = jnp.float32
    x, z, core = place_ref[1], place_ref[2], place_ref[3]

    def fetch(step):
        r = pl.ds(pl.multiple_of(step * ROWS_STEP, ROWS_STEP), ROWS_STEP)
        return pltpu.make_async_copy(e_ref.at[r], held.at[r], sem.at[step])

    @pl.when(i == 0)
    def _():
        table = pltpu.make_async_copy(t_ref, t_held, t_sem)
        table.start()
        fetch(0).start()
        table.wait()
        fetch(1).start()

    @pl.when(i < steps)
    def _():
        fetch(i).wait()

        @pl.when(i + 2 < steps)
        def _():
            fetch(i + 2).start()

        r = pl.ds(pl.multiple_of(i * ROWS_STEP, ROWS_STEP), ROWS_STEP)
        s = jnp.dot(held[r, :], t_held[...], preferred_element_type=f32)
        hi = s.astype(jnp.bfloat16)
        s_ref[r, 0:K] = hi
        s_ref[r, K : 2 * K] = (s - hi.astype(f32)).astype(jnp.bfloat16)

    @pl.when(i == steps)
    def _():
        g = lax.dot_general(
            s_ref[:, 0:K], s_ref[...], OVER_ROWS, preferred_element_type=f32
        )
        mixed = g[:, K : 2 * K]
        gram[...] = g[:, 0:K] + (mixed + mixed.T)

        def pack(out, c):
            diagonal = gram[c * HALF : (c + 1) * HALF, c * HALF : (c + 1) * HALF]
            below = gram[HALF + 64 * c : HALF + 64 * (c + 1), 0:HALF]
            out[:, :, 0:HALF] = diagonal[0:96].reshape(PACKED, 32, HALF)
            out[0, :, HALF:K] = diagonal[96:128]
            out[1:3, :, HALF:K] = below.reshape(2, 32, HALF)

        @pl.when(core == 0)
        def _():
            pack(gram_keep_ref, 0)
            pack(gram_send_ref, 1)

        @pl.when(core != 0)
        def _():
            pack(gram_keep_ref, 1)
            pack(gram_send_ref, 0)

    @pl.when(i >= steps)
    def _():
        c = pl.ds(pl.multiple_of((i - steps) * COLS_STEP, COLS_STEP), COLS_STEP)
        m = lax.dot_general(held[:, c], s_ref[...], OVER_ROWS, preferred_element_type=f32)
        parts[...] = (m[:, 0:K] + m[:, K : 2 * K]).reshape(CHIPS_STEP, 2, 32, K)
        for k, send_ref in enumerate((s0, s1, s2, s3)):
            for o in range(4):
                by_z = 4 * o + ((z + k) & 3)
                by_x = 4 * ((x + k) & 3) + o
                keep_ref[k, 0, o] = parts[jnp.where(core == 0, by_z, by_x), core]
                send_ref[0, o] = parts[jnp.where(core == 0, by_x, by_z), 1 - core]


def blocks(*lead):
    return jax.ShapeDtypeStruct(lead + (32, K), jnp.float32)


def local_products(place, e, t):
    rows, d = e.shape
    steps = rows // ROWS_STEP

    def column(i):
        return jnp.maximum(i - steps, 0)

    kept = pl.BlockSpec((4, 1, 4, 32, K), lambda i: (0, column(i), 0, 0, 0))
    sent = pl.BlockSpec((1, 4, 32, K), lambda i: (column(i), 0, 0, 0))
    whole = pl.BlockSpec((PACKED, 32, K), lambda i: (0, 0, 0))
    return pl.pallas_call(
        functools.partial(local_kernel, steps),
        grid_spec=pl.GridSpec(
            grid=(steps + d // COLS_STEP,),
            in_specs=[
                pl.BlockSpec(memory_space=pltpu.SMEM),
                pl.BlockSpec(memory_space=pl.ANY),
                pl.BlockSpec(memory_space=pl.ANY),
            ],
            out_specs=[kept] + [sent] * 4 + [whole] * 2,
            scratch_shapes=[
                pltpu.VMEM((rows, d), jnp.bfloat16),
                pltpu.VMEM((d, K), jnp.bfloat16),
                pltpu.VMEM((rows, 2 * K), jnp.bfloat16),
                pltpu.VMEM((K, K), jnp.float32),
                pltpu.VMEM((CHIPS_STEP, 2, 32, K), jnp.float32),
                pltpu.SemaphoreType.DMA((steps,)),
                pltpu.SemaphoreType.DMA,
            ],
        ),
        out_shape=[blocks(4, 4, 4)] + [blocks(4, 4)] * 4 + [blocks(PACKED)] * 2,
        compiler_params=pltpu.CompilerParams(vmem_limit_bytes=46 * MIB),
        cost_estimate=pl.CostEstimate(
            flops=6 * rows * K * d + 8 * rows * K * K,
            bytes_accessed=rows * d * 2 + d * K * 6,
            transcendentals=0,
        ),
        name="local_products",
    )(place, e, pltpu.with_memory_space_constraint(t, pltpu.HBM))


def one_step(kernel, name, out_shape):
    vmem = pl.BlockSpec(memory_space=pltpu.VMEM)

    def call(*args, scratch=()):
        return pl.pallas_call(
            kernel,
            out_shape=out_shape,
            in_specs=[vmem] * len(args),
            out_specs=[vmem] * len(out_shape),
            scratch_shapes=list(scratch),
            compiler_params=pltpu.CompilerParams(vmem_limit_bytes=20 * MIB),
            name=name,
        )(*args)

    return call


def message_kernel(k, keep_ref, got_ref, gk_ref, gg_ref, out_ref):
    out_ref[0:16] = (keep_ref[k] + got_ref[...]).reshape(16, 32, K)
    out_ref[16:] = gk_ref[...] + gg_ref[...]


def message(k, keep, got, gk, gg):
    kernel = functools.partial(message_kernel, k)
    return one_step(kernel, "message", [blocks(16 + PACKED)])(keep, got, gk, gg)[0]


def second_kernel(keep_ref, got_ref, gk_ref, gg_ref, a, b, c, own, *refs):
    out, m = refs[:-1], refs[-1]
    core = lax.axis_index("core")
    y, z = lax.axis_index("y"), lax.axis_index("z")
    m[...] = (keep_ref[0] + got_ref[...]) + (a[0:16] + b[0:16] + c[0:16]).reshape(
        4, 4, 32, K
    )
    gram = (gk_ref[...] + gg_ref[...]) + (a[16:] + b[16:] + c[16:])
    for ref, k in zip((own,) + out, (0,) + DISTANCES):
        for i in range(4):
            first = jnp.where(core == 0, (y + k) & 3, i)
            other = jnp.where(core == 0, i, (z + k) & 3)
            ref[i] = m[first, other]
    for ref in out:
        ref[4:] = gram


def second(keep, got, gk, gg, arrived):
    outs = [blocks(4)] + [blocks(4 + PACKED)] * 3
    scratch = [pltpu.VMEM((4, 4, 32, K), jnp.float32)]
    return one_step(second_kernel, "second", outs)(
        keep, got, gk, gg, *arrived, scratch=scratch
    )


def third_kernel(own_ref, sent, a, b, c, own, *refs):
    out, m = refs[:-1], refs[-1]
    m[...] = own_ref[...] + (a[0:4] + b[0:4] + c[0:4])
    gram = sent[4:] + (a[4:] + b[4:] + c[4:])
    at = jnp.where(lax.axis_index("core") == 0, lax.axis_index("x"), lax.axis_index("y"))
    own[...] = m[at]
    for ref, k in zip(out, DISTANCES):
        ref[0] = m[(at + k) & 3]
        ref[1:] = gram


def third(own, sent, arrived):
    outs = [blocks()] + [blocks(1 + PACKED)] * 3
    scratch = [pltpu.VMEM((4, 32, K), jnp.float32)]
    return one_step(third_kernel, "third", outs)(own, sent, *arrived, scratch=scratch)


def last_kernel(own_ref, sent, a, b, c, m_ref, g_ref):
    m_ref[...] = own_ref[...] + (a[0] + b[0] + c[0])
    g_ref[...] = sent[1:] + (a[1:] + b[1:] + c[1:])


def last(own, sent, arrived):
    return one_step(last_kernel, "last", [blocks(), blocks(PACKED)])(own, sent, *arrived)


def across(v, lane):
    return jnp.take_along_axis(v, jnp.full(v.shape, lane, jnp.int32), axis=1)


def chol_inverse(x):
    lane = lax.broadcasted_iota(jnp.int32, (B, HALF), 1)
    n = HALF // B
    for j in range(n):
        o = j * B
        inside = (lane >= o) & (lane < o + B)
        panel = x[o : o + B, :]
        cols = [across(panel, o + b) for b in range(B)]
        d = [
            [jnp.broadcast_to(cols[b][a : a + 1, :], (B, HALF)) for b in range(a + 1)]
            for a in range(B)
        ]
        rows = []
        for a in range(B):
            r = jnp.broadcast_to(x[o + a : o + a + 1, :], (B, HALF))
            rows.append(jnp.where(inside, jnp.where(lane == o + a, 1.0, 0.0), r))
        more = j + 1 < n
        if more:
            old = x[o + B : o + 2 * B, :]
            c = [across(old, o + k) for k in range(B)]
            following = jnp.where(inside, 0.0, old)
        l = [[None] * B for _ in range(B)]
        scale, v = [], []
        for i in range(B):
            inv = lax.rsqrt(d[i][i])
            scale.append(inv)
            for a in range(i + 1, B):
                l[a][i] = d[a][i] * inv
            for a in range(i + 1, B):
                for b in range(i + 1, a + 1):
                    d[a][b] = d[a][b] - l[a][i] * l[b][i]
            v.append(rows[i] * inv)
            for a in range(i + 1, B):
                rows[a] = rows[a] - l[a][i] * v[i]
            if more:
                scaled = c[i] * inv
                for a in range(i + 1, B):
                    c[a] = c[a] - l[a][i] * scaled
                following = following - scaled * v[i]
        if more:
            x[o + B : o + 2 * B, :] = following
        if j + 2 < n:
            y = [None] * B
            for i in reversed(range(B)):
                t = v[i]
                for a in range(i + 1, B):
                    t = t - l[a][i] * y[a]
                y[i] = t * scale[i]
            for r in range(j + 2, n):
                sl = slice(r * B, (r + 1) * B)
                old = x[sl, :]
                c = [across(old, o + k) for k in range(B)]
                x[sl, :] = jnp.where(inside, 0.0, old) - tree([c[k] * y[k] for k in range(B)])
        for i in range(B):
            x[o + i : o + i + 1, :] = jnp.where(lane < o + B, v[i], 0.0)[0:1, :]


def times_transposed(a, b):
    return lax.dot_general(
        a,
        b,
        (((1,), (1,)), ((), ())),
        precision=lax.Precision.HIGHEST,
        preferred_element_type=jnp.float32,
    )


def finish_kernel(m_ref, own_ref, other_ref, out_ref, a, b):
    core = lax.axis_index("core")
    zero = jnp.where(core == 0, own_ref[...], other_ref[...])
    one = jnp.where(core == 0, other_ref[...], own_ref[...])

    def unpack(packed):
        left = packed[:, :, 0:HALF].reshape(96, HALF)
        right = packed[:, :, HALF:K].reshape(96, HALF)
        return jnp.concatenate([left, right[0:32]], axis=0), right[32:96]

    a[...], upper = unpack(zero)
    corner, lower = unpack(one)
    below = jnp.concatenate([upper, lower], axis=0)
    chol_inverse(a)
    factor = times_transposed(below, a[...])
    b[...] = corner - times_transposed(factor, factor)
    first = times_transposed(m_ref[:, 0:HALF], a[...])
    rest = m_ref[:, HALF:K] - times_transposed(first, factor)
    chol_inverse(b)
    out_ref[:, 0:HALF] = first
    out_ref[:, HALF:K] = times_transposed(rest, b[...])


def finish(m, own, other):
    vmem = pl.BlockSpec(memory_space=pltpu.VMEM)
    return pl.pallas_call(
        finish_kernel,
        out_shape=blocks(),
        in_specs=[vmem] * 3,
        out_specs=vmem,
        scratch_shapes=[pltpu.VMEM((HALF, HALF), jnp.float32)] * 2,
        compiler_params=pltpu.CompilerParams(vmem_limit_bytes=32 * MIB),
        name="finish",
    )(m, own, other)


DISTANCES = (2, 1, 3)


def ring_pairs(axes, distance):
    pairs = []
    for source in range(128):
        place = {"y": source // 32, "x": source // 8 % 4, "z": source // 2 % 4}
        core = source % 2
        place[axes[core]] = (place[axes[core]] + distance) % 4
        target = ((place["y"] * 4 + place["x"]) * 4 + place["z"]) * 2 + core
        pairs.append((source, target))
    return pairs


def solution(mesh):
    every = ("y", "x", "z", "core")
    fine = Mesh(mesh.devices.reshape(4, 4, 4, 2), every)
    swap = [(0, 1), (1, 0)]

    def along(axes, messages):
        return [
            lax.ppermute(m, every, ring_pairs(axes, k)) for m, k in zip(messages, DISTANCES)
        ]

    def local(embedding, test_matrix):
        place = jnp.stack([lax.axis_index(a) for a in every]).astype(jnp.int32)
        keep, *send, gk, gs = local_products(place, embedding, test_matrix)
        got = [None] * 4
        got[2] = lax.ppermute(send[2], "core", swap)
        gg = lax.ppermute(gs, "core", swap)
        send[1], send[3], send[0], gg = lax.optimization_barrier(
            (send[1], send[3], send[0], gg)
        )
        for k in (1, 3, 0):
            got[k] = lax.ppermute(send[k], "core", swap)
        messages = [message(k, keep, got[k], gk, gg) for k in DISTANCES]
        arrived = along(("z", "x"), messages)
        own, *messages = second(keep, got[0], gk, gg, arrived)
        arrived = along(("y", "z"), messages)
        own, *messages_3 = third(own, messages[0], arrived)
        arrived = along(("x", "y"), messages_3)
        m, g = last(own, messages_3[0], arrived)
        return finish(m, g, lax.ppermute(g, "core", swap))

    return jax.shard_map(
        local,
        mesh=fine,
        in_specs=(P(every, None), P()),
        out_specs=P(every, None),
        check_vma=False,
    )
```

```python
import functools

import jax
import jax.numpy as jnp
from jax import lax
from jax.experimental import pallas as pl
from jax.experimental.pallas import tpu as pltpu
from jax.sharding import Mesh, PartitionSpec as P

K = 256
B = 8
HALF = K // 2
MIB = 1 << 20


def tree(terms):
    while len(terms) > 1:
        terms = [
            terms[i] + terms[i + 1] if i + 1 < len(terms) else terms[i]
            for i in range(0, len(terms), 2)
        ]
    return terms[0]


ROWS_STEP = 768
COLS_STEP = 1024
CHIPS_STEP = COLS_STEP // 64
PACKED = 80
OVER_ROWS = (((0,), (0,)), ((), ()))


def local_kernel(
    steps, place_ref, e_ref, t_ref, keep_ref, s0, s1, s2, s3, gram_keep_ref,
    gram_send_ref, held, t_held, s_ref, gram, parts, sem, t_sem,
):
    i = pl.program_id(0)
    f32 = jnp.float32
    x, z, core = place_ref[1], place_ref[2], place_ref[3]

    def fetch(step):
        r = pl.ds(pl.multiple_of(step * ROWS_STEP, ROWS_STEP), ROWS_STEP)
        return pltpu.make_async_copy(e_ref.at[r], held.at[r], sem.at[step])

    @pl.when(i == 0)
    def _():
        table = pltpu.make_async_copy(t_ref, t_held, t_sem)
        table.start()
        fetch(0).start()
        table.wait()
        fetch(1).start()

    @pl.when(i < steps)
    def _():
        fetch(i).wait()

        @pl.when(i + 2 < steps)
        def _():
            fetch(i + 2).start()

        r = pl.ds(pl.multiple_of(i * ROWS_STEP, ROWS_STEP), ROWS_STEP)
        s = jnp.dot(held[r, :], t_held[...], preferred_element_type=f32)
        hi = s.astype(jnp.bfloat16)
        s_ref[r, 0:K] = hi
        s_ref[r, K : 2 * K] = (s - hi.astype(f32)).astype(jnp.bfloat16)

    @pl.when(i == steps)
    def _():
        g = lax.dot_general(
            s_ref[:, 0:K], s_ref[...], OVER_ROWS, preferred_element_type=f32
        )
        mixed = g[:, K : 2 * K]
        gram[...] = g[:, 0:K] + (mixed + mixed.T)

        def pack(out, c):
            own = slice(c * HALF, (c + 1) * HALF)
            diagonal = gram[own, own]
            out[0:64, 0:HALF] = gram[HALF + 64 * c : HALF + 64 * (c + 1), 0:HALF]
            out[0:64, HALF:K] = diagonal[64:HALF]
            corner = diagonal[0:64, 0:64]
            out[64:PACKED, :] = jnp.concatenate(
                [corner[16 * q : 16 * (q + 1)] for q in range(4)], axis=1
            )

        @pl.when(core == 0)
        def _():
            pack(gram_keep_ref, 0)
            pack(gram_send_ref, 1)

        @pl.when(core != 0)
        def _():
            pack(gram_keep_ref, 1)
            pack(gram_send_ref, 0)

    @pl.when(i >= steps)
    def _():
        c = pl.ds(pl.multiple_of((i - steps) * COLS_STEP, COLS_STEP), COLS_STEP)
        m = lax.dot_general(held[:, c], s_ref[...], OVER_ROWS, preferred_element_type=f32)
        parts[...] = (m[:, 0:K] + m[:, K : 2 * K]).reshape(CHIPS_STEP, 2, 32, K)
        for k, send_ref in enumerate((s0, s1, s2, s3)):
            for o in range(4):
                by_z = 4 * o + ((z + k) & 3)
                by_x = 4 * ((x + k) & 3) + o
                keep_ref[k, 0, o] = parts[jnp.where(core == 0, by_z, by_x), core]
                send_ref[0, o] = parts[jnp.where(core == 0, by_x, by_z), 1 - core]


def blocks(*lead):
    return jax.ShapeDtypeStruct(lead + (32, K), jnp.float32)


def flat(n):
    return jax.ShapeDtypeStruct((32 * n + PACKED, K), jnp.float32)


def local_products(place, e, t):
    rows, d = e.shape
    steps = rows // ROWS_STEP

    def column(i):
        return jnp.maximum(i - steps, 0)

    kept = pl.BlockSpec((4, 1, 4, 32, K), lambda i: (0, column(i), 0, 0, 0))
    sent = pl.BlockSpec((1, 4, 32, K), lambda i: (column(i), 0, 0, 0))
    whole = pl.BlockSpec((PACKED, K), lambda i: (0, 0))
    return pl.pallas_call(
        functools.partial(local_kernel, steps),
        grid_spec=pl.GridSpec(
            grid=(steps + d // COLS_STEP,),
            in_specs=[
                pl.BlockSpec(memory_space=pltpu.SMEM),
                pl.BlockSpec(memory_space=pl.ANY),
                pl.BlockSpec(memory_space=pl.ANY),
            ],
            out_specs=[kept] + [sent] * 4 + [whole] * 2,
            scratch_shapes=[
                pltpu.VMEM((rows, d), jnp.bfloat16),
                pltpu.VMEM((d, K), jnp.bfloat16),
                pltpu.VMEM((rows, 2 * K), jnp.bfloat16),
                pltpu.VMEM((K, K), jnp.float32),
                pltpu.VMEM((CHIPS_STEP, 2, 32, K), jnp.float32),
                pltpu.SemaphoreType.DMA((steps,)),
                pltpu.SemaphoreType.DMA,
            ],
        ),
        out_shape=[blocks(4, 4, 4)] + [blocks(4, 4)] * 4 + [flat(0)] * 2,
        compiler_params=pltpu.CompilerParams(vmem_limit_bytes=46 * MIB),
        cost_estimate=pl.CostEstimate(
            flops=6 * rows * K * d + 8 * rows * K * K,
            bytes_accessed=rows * d * 2 + d * K * 6,
            transcendentals=0,
        ),
        name="local_products",
    )(place, e, pltpu.with_memory_space_constraint(t, pltpu.HBM))


def one_step(kernel, name, out_shape):
    vmem = pl.BlockSpec(memory_space=pltpu.VMEM)

    def call(*args, scratch=()):
        return pl.pallas_call(
            kernel,
            out_shape=out_shape,
            in_specs=[vmem] * len(args),
            out_specs=[vmem] * len(out_shape),
            scratch_shapes=list(scratch),
            compiler_params=pltpu.CompilerParams(vmem_limit_bytes=20 * MIB),
            name=name,
        )(*args)

    return call


def message_kernel(k, keep_ref, got_ref, gk_ref, gg_ref, out_ref):
    out_ref[0:512] = (keep_ref[k] + got_ref[...]).reshape(512, K)
    out_ref[512:] = gk_ref[...] + gg_ref[...]


def message(k, keep, got, gk, gg):
    kernel = functools.partial(message_kernel, k)
    return one_step(kernel, "message", [flat(16)])(keep, got, gk, gg)[0]


def second_kernel(keep_ref, got_ref, gk_ref, gg_ref, a, b, c, own, *refs):
    out, m = refs[:-1], refs[-1]
    core = lax.axis_index("core")
    y, z = lax.axis_index("y"), lax.axis_index("z")
    m[...] = (keep_ref[0] + got_ref[...]) + (a[0:512] + b[0:512] + c[0:512]).reshape(
        4, 4, 32, K
    )
    gram = (gk_ref[...] + gg_ref[...]) + (a[512:] + b[512:] + c[512:])
    for ref, k in zip((own,) + out, (0,) + DISTANCES):
        for i in range(4):
            first = jnp.where(core == 0, (y + k) & 3, i)
            other = jnp.where(core == 0, i, (z + k) & 3)
            ref[32 * i : 32 * (i + 1)] = m[first, other]
    for ref in out:
        ref[128:] = gram


def second(keep, got, gk, gg, arrived):
    outs = [jax.ShapeDtypeStruct((128, K), jnp.float32)] + [flat(4)] * 3
    scratch = [pltpu.VMEM((4, 4, 32, K), jnp.float32)]
    return one_step(second_kernel, "second", outs)(
        keep, got, gk, gg, *arrived, scratch=scratch
    )


def third_kernel(own_ref, sent, a, b, c, own, *refs):
    out, m = refs[:-1], refs[-1]
    m[...] = (own_ref[...] + (a[0:128] + b[0:128] + c[0:128])).reshape(4, 32, K)
    gram = sent[128:] + (a[128:] + b[128:] + c[128:])
    at = jnp.where(lax.axis_index("core") == 0, lax.axis_index("x"), lax.axis_index("y"))
    own[...] = m[at]
    for ref, k in zip(out, DISTANCES):
        ref[0:32] = m[(at + k) & 3]
        ref[32:] = gram


def third(own, sent, arrived):
    outs = [blocks()] + [flat(1)] * 3
    scratch = [pltpu.VMEM((4, 32, K), jnp.float32)]
    return one_step(third_kernel, "third", outs)(own, sent, *arrived, scratch=scratch)


def last_kernel(own_ref, sent, a, b, c, m_ref, g_ref):
    m_ref[...] = own_ref[...] + (a[0:32] + b[0:32] + c[0:32])
    g_ref[...] = sent[32:] + (a[32:] + b[32:] + c[32:])


def last(own, sent, arrived):
    return one_step(last_kernel, "last", [blocks(), flat(0)])(own, sent, *arrived)


def across(v, lane):
    return jnp.take_along_axis(v, jnp.full(v.shape, lane, jnp.int32), axis=1)


def chol_inverse(x):
    lane = lax.broadcasted_iota(jnp.int32, (B, HALF), 1)
    n = HALF // B
    for j in range(n):
        o = j * B
        inside = (lane >= o) & (lane < o + B)
        panel = x[o : o + B, :]
        cols = [across(panel, o + b) for b in range(B)]
        d = [
            [jnp.broadcast_to(cols[b][a : a + 1, :], (B, HALF)) for b in range(a + 1)]
            for a in range(B)
        ]
        rows = []
        for a in range(B):
            r = jnp.broadcast_to(x[o + a : o + a + 1, :], (B, HALF))
            rows.append(jnp.where(inside, jnp.where(lane == o + a, 1.0, 0.0), r))
        more = j + 1 < n
        if more:
            old = x[o + B : o + 2 * B, :]
            c = [across(old, o + k) for k in range(B)]
            following = jnp.where(inside, 0.0, old)
        l = [[None] * B for _ in range(B)]
        scale, v = [], []
        for i in range(B):
            inv = lax.rsqrt(d[i][i])
            scale.append(inv)
            for a in range(i + 1, B):
                l[a][i] = d[a][i] * inv
            for a in range(i + 1, B):
                for b in range(i + 1, a + 1):
                    d[a][b] = d[a][b] - l[a][i] * l[b][i]
            v.append(rows[i] * inv)
            for a in range(i + 1, B):
                rows[a] = rows[a] - l[a][i] * v[i]
            if more:
                scaled = c[i] * inv
                for a in range(i + 1, B):
                    c[a] = c[a] - l[a][i] * scaled
                following = following - scaled * v[i]
        if more:
            x[o + B : o + 2 * B, :] = following
        if j + 2 < n:
            y = [None] * B
            for i in reversed(range(B)):
                t = v[i]
                for a in range(i + 1, B):
                    t = t - l[a][i] * y[a]
                y[i] = t * scale[i]
            for r in range(j + 2, n):
                sl = slice(r * B, (r + 1) * B)
                old = x[sl, :]
                c = [across(old, o + k) for k in range(B)]
                x[sl, :] = jnp.where(inside, 0.0, old) - tree([c[k] * y[k] for k in range(B)])
        for i in range(B):
            x[o + i : o + i + 1, :] = jnp.where(lane < o + B, v[i], 0.0)[0:1, :]


def times_transposed(a, b):
    return lax.dot_general(
        a,
        b,
        (((1,), (1,)), ((), ())),
        precision=lax.Precision.HIGHEST,
        preferred_element_type=jnp.float32,
    )


def finish_kernel(m_ref, own_ref, other_ref, out_ref, a, b):
    core = lax.axis_index("core")
    zero = jnp.where(core == 0, own_ref[...], other_ref[...])
    one = jnp.where(core == 0, other_ref[...], own_ref[...])

    def unpack(packed):
        low = packed[0:64, HALF:K]
        corner = [packed[64:PACKED, 64 * q : 64 * (q + 1)] for q in range(4)]
        top = jnp.concatenate([jnp.concatenate(corner, axis=0), low[:, 0:64].T], axis=1)
        return jnp.concatenate([top, low], axis=0), packed[0:64, 0:HALF]

    a[...], upper = unpack(zero)
    corner, lower = unpack(one)
    below = jnp.concatenate([upper, lower], axis=0)
    chol_inverse(a)
    factor = times_transposed(below, a[...])
    b[...] = corner - times_transposed(factor, factor)
    first = times_transposed(m_ref[:, 0:HALF], a[...])
    rest = m_ref[:, HALF:K] - times_transposed(first, factor)
    chol_inverse(b)
    out_ref[:, 0:HALF] = first
    out_ref[:, HALF:K] = times_transposed(rest, b[...])


def finish(m, own, other):
    vmem = pl.BlockSpec(memory_space=pltpu.VMEM)
    return pl.pallas_call(
        finish_kernel,
        out_shape=blocks(),
        in_specs=[vmem] * 3,
        out_specs=vmem,
        scratch_shapes=[pltpu.VMEM((HALF, HALF), jnp.float32)] * 2,
        compiler_params=pltpu.CompilerParams(vmem_limit_bytes=32 * MIB),
        name="finish",
    )(m, own, other)


DISTANCES = (2, 1, 3)


def ring_pairs(axes, distance):
    pairs = []
    for source in range(128):
        place = {"y": source // 32, "x": source // 8 % 4, "z": source // 2 % 4}
        core = source % 2
        place[axes[core]] = (place[axes[core]] + distance) % 4
        target = ((place["y"] * 4 + place["x"]) * 4 + place["z"]) * 2 + core
        pairs.append((source, target))
    return pairs


def solution(mesh):
    every = ("y", "x", "z", "core")
    fine = Mesh(mesh.devices.reshape(4, 4, 4, 2), every)
    swap = [(0, 1), (1, 0)]

    def along(axes, messages):
        return [
            lax.ppermute(m, every, ring_pairs(axes, k)) for m, k in zip(messages, DISTANCES)
        ]

    def local(embedding, test_matrix):
        place = jnp.stack([lax.axis_index(a) for a in every]).astype(jnp.int32)
        keep, *send, gk, gs = local_products(place, embedding, test_matrix)
        got = [None] * 4
        got[2] = lax.ppermute(send[2], "core", swap)
        gg = lax.ppermute(gs, "core", swap)
        send[1], send[3], send[0], gg = lax.optimization_barrier(
            (send[1], send[3], send[0], gg)
        )
        for k in (1, 3, 0):
            got[k] = lax.ppermute(send[k], "core", swap)
        messages = [message(k, keep, got[k], gk, gg) for k in DISTANCES]
        arrived = along(("z", "x"), messages)
        own, *messages = second(keep, got[0], gk, gg, arrived)
        arrived = along(("y", "z"), messages)
        own, *messages_3 = third(own, messages[0], arrived)
        arrived = along(("x", "y"), messages_3)
        m, g = last(own, messages_3[0], arrived)
        return finish(m, g, lax.ppermute(g, "core", swap))

    return jax.shard_map(
        local,
        mesh=fine,
        in_specs=(P(every, None), P()),
        out_specs=P(every, None),
        check_vma=False,
    )
```

```python
import functools

import jax
import jax.numpy as jnp
from jax import lax
from jax.experimental import pallas as pl
from jax.experimental.pallas import tpu as pltpu
from jax.sharding import Mesh, PartitionSpec as P

K = 256
B = 8
HALF = K // 2
MIB = 1 << 20


def tree(terms):
    while len(terms) > 1:
        terms = [
            terms[i] + terms[i + 1] if i + 1 < len(terms) else terms[i]
            for i in range(0, len(terms), 2)
        ]
    return terms[0]


ROWS_STEP = 512
COLS_STEP = 1024
CHIPS_STEP = COLS_STEP // 64
PACKED = 80
OVER_ROWS = (((0,), (0,)), ((), ()))


def local_kernel(
    steps, place_ref, e_ref, t_ref, keep_ref, s0, s1, s2, s3, gram_keep_ref,
    gram_send_ref, held, t_held, s_ref, gram, parts, sem, t_sem,
):
    i = pl.program_id(0)
    f32 = jnp.float32
    x, z, core = place_ref[1], place_ref[2], place_ref[3]

    def fetch(step):
        r = pl.ds(pl.multiple_of(step * ROWS_STEP, ROWS_STEP), ROWS_STEP)
        return pltpu.make_async_copy(e_ref.at[r], held.at[r], sem.at[step])

    @pl.when(i == 0)
    def _():
        table = pltpu.make_async_copy(t_ref, t_held, t_sem)
        table.start()
        fetch(0).start()
        table.wait()
        fetch(1).start()

        def sketch(step, carry):
            fetch(step).wait()

            @pl.when(step + 2 < steps)
            def _():
                fetch(step + 2).start()

            r = pl.ds(pl.multiple_of(step * ROWS_STEP, ROWS_STEP), ROWS_STEP)
            s = jnp.dot(held[r, :], t_held[...], preferred_element_type=f32)
            hi = s.astype(jnp.bfloat16)
            s_ref[r, 0:K] = hi
            s_ref[r, K : 2 * K] = (s - hi.astype(f32)).astype(jnp.bfloat16)
            return carry

        lax.fori_loop(0, steps, sketch, 0)
        g = lax.dot_general(
            s_ref[:, 0:K], s_ref[...], OVER_ROWS, preferred_element_type=f32
        )
        mixed = g[:, K : 2 * K]
        gram[...] = g[:, 0:K] + (mixed + mixed.T)

        def pack(out, c):
            own = slice(c * HALF, (c + 1) * HALF)
            diagonal = gram[own, own]
            out[0:64, 0:HALF] = gram[HALF + 64 * c : HALF + 64 * (c + 1), 0:HALF]
            out[0:64, HALF:K] = diagonal[64:HALF]
            corner = diagonal[0:64, 0:64]
            out[64:PACKED, :] = jnp.concatenate(
                [corner[16 * q : 16 * (q + 1)] for q in range(4)], axis=1
            )

        @pl.when(core == 0)
        def _():
            pack(gram_keep_ref, 0)
            pack(gram_send_ref, 1)

        @pl.when(core != 0)
        def _():
            pack(gram_keep_ref, 1)
            pack(gram_send_ref, 0)

    @pl.when(i > 0)
    def _():
        c = pl.ds(pl.multiple_of((i - 1) * COLS_STEP, COLS_STEP), COLS_STEP)
        m = lax.dot_general(held[:, c], s_ref[...], OVER_ROWS, preferred_element_type=f32)
        parts[...] = (m[:, 0:K] + m[:, K : 2 * K]).reshape(CHIPS_STEP, 2, 32, K)
        for k, send_ref in enumerate((s0, s1, s2, s3)):
            for o in range(4):
                by_z = 4 * o + ((z + k) & 3)
                by_x = 4 * ((x + k) & 3) + o
                keep_ref[k, 0, o] = parts[jnp.where(core == 0, by_z, by_x), core]
                send_ref[0, o] = parts[jnp.where(core == 0, by_x, by_z), 1 - core]


def blocks(*lead):
    return jax.ShapeDtypeStruct(lead + (32, K), jnp.float32)


def flat(n):
    return jax.ShapeDtypeStruct((32 * n + PACKED, K), jnp.float32)


def local_products(place, e, t):
    rows, d = e.shape
    steps = rows // ROWS_STEP

    def column(i):
        return jnp.maximum(i - 1, 0)

    kept = pl.BlockSpec((4, 1, 4, 32, K), lambda i: (0, column(i), 0, 0, 0))
    sent = pl.BlockSpec((1, 4, 32, K), lambda i: (column(i), 0, 0, 0))
    whole = pl.BlockSpec((PACKED, K), lambda i: (0, 0))
    return pl.pallas_call(
        functools.partial(local_kernel, steps),
        grid_spec=pl.GridSpec(
            grid=(1 + d // COLS_STEP,),
            in_specs=[
                pl.BlockSpec(memory_space=pltpu.SMEM),
                pl.BlockSpec(memory_space=pl.ANY),
                pl.BlockSpec(memory_space=pl.ANY),
            ],
            out_specs=[kept] + [sent] * 4 + [whole] * 2,
            scratch_shapes=[
                pltpu.VMEM((rows, d), jnp.bfloat16),
                pltpu.VMEM((d, K), jnp.bfloat16),
                pltpu.VMEM((rows, 2 * K), jnp.bfloat16),
                pltpu.VMEM((K, K), jnp.float32),
                pltpu.VMEM((CHIPS_STEP, 2, 32, K), jnp.float32),
                pltpu.SemaphoreType.DMA((steps,)),
                pltpu.SemaphoreType.DMA,
            ],
        ),
        out_shape=[blocks(4, 4, 4)] + [blocks(4, 4)] * 4 + [flat(0)] * 2,
        compiler_params=pltpu.CompilerParams(vmem_limit_bytes=46 * MIB),
        cost_estimate=pl.CostEstimate(
            flops=6 * rows * K * d + 8 * rows * K * K,
            bytes_accessed=rows * d * 2 + d * K * 6,
            transcendentals=0,
        ),
        name="local_products",
    )(place, e, pltpu.with_memory_space_constraint(t, pltpu.HBM))


def one_step(kernel, name, out_shape):
    vmem = pl.BlockSpec(memory_space=pltpu.VMEM)

    def call(*args, scratch=()):
        return pl.pallas_call(
            kernel,
            out_shape=out_shape,
            in_specs=[vmem] * len(args),
            out_specs=[vmem] * len(out_shape),
            scratch_shapes=list(scratch),
            compiler_params=pltpu.CompilerParams(vmem_limit_bytes=20 * MIB),
            name=name,
        )(*args)

    return call


def message_kernel(k, keep_ref, got_ref, gk_ref, gg_ref, out_ref):
    out_ref[0:512] = (keep_ref[k] + got_ref[...]).reshape(512, K)
    out_ref[512:] = gk_ref[...] + gg_ref[...]


def message(k, keep, got, gk, gg):
    kernel = functools.partial(message_kernel, k)
    return one_step(kernel, "message", [flat(16)])(keep, got, gk, gg)[0]


def second_kernel(keep_ref, got_ref, gk_ref, gg_ref, a, b, c, own, *refs):
    out, m = refs[:-1], refs[-1]
    core = lax.axis_index("core")
    y, z = lax.axis_index("y"), lax.axis_index("z")
    m[...] = (keep_ref[0] + got_ref[...]) + (a[0:512] + b[0:512] + c[0:512]).reshape(
        4, 4, 32, K
    )
    gram = (gk_ref[...] + gg_ref[...]) + (a[512:] + b[512:] + c[512:])
    for ref, k in zip((own,) + out, (0,) + DISTANCES):
        for i in range(4):
            first = jnp.where(core == 0, (y + k) & 3, i)
            other = jnp.where(core == 0, i, (z + k) & 3)
            ref[32 * i : 32 * (i + 1)] = m[first, other]
    for ref in out:
        ref[128:] = gram


def second(keep, got, gk, gg, arrived):
    outs = [jax.ShapeDtypeStruct((128, K), jnp.float32)] + [flat(4)] * 3
    scratch = [pltpu.VMEM((4, 4, 32, K), jnp.float32)]
    return one_step(second_kernel, "second", outs)(
        keep, got, gk, gg, *arrived, scratch=scratch
    )


def third_kernel(own_ref, sent, a, b, c, own, *refs):
    out, m = refs[:-1], refs[-1]
    m[...] = (own_ref[...] + (a[0:128] + b[0:128] + c[0:128])).reshape(4, 32, K)
    gram = sent[128:] + (a[128:] + b[128:] + c[128:])
    at = jnp.where(lax.axis_index("core") == 0, lax.axis_index("x"), lax.axis_index("y"))
    own[...] = m[at]
    for ref, k in zip(out, DISTANCES):
        ref[0:32] = m[(at + k) & 3]
        ref[32:] = gram


def third(own, sent, arrived):
    outs = [blocks()] + [flat(1)] * 3
    scratch = [pltpu.VMEM((4, 32, K), jnp.float32)]
    return one_step(third_kernel, "third", outs)(own, sent, *arrived, scratch=scratch)


def last_kernel(own_ref, sent, a, b, c, m_ref, g_ref):
    m_ref[...] = own_ref[...] + (a[0:32] + b[0:32] + c[0:32])
    g_ref[...] = sent[32:] + (a[32:] + b[32:] + c[32:])


def last(own, sent, arrived):
    return one_step(last_kernel, "last", [blocks(), flat(0)])(own, sent, *arrived)


def across(v, lane):
    return jnp.take_along_axis(v, jnp.full(v.shape, lane, jnp.int32), axis=1)


def chol_inverse(x):
    lane = lax.broadcasted_iota(jnp.int32, (B, HALF), 1)
    n = HALF // B
    for j in range(n):
        o = j * B
        inside = (lane >= o) & (lane < o + B)
        panel = x[o : o + B, :]
        cols = [across(panel, o + b) for b in range(B)]
        d = [
            [jnp.broadcast_to(cols[b][a : a + 1, :], (B, HALF)) for b in range(a + 1)]
            for a in range(B)
        ]
        rows = []
        for a in range(B):
            r = jnp.broadcast_to(x[o + a : o + a + 1, :], (B, HALF))
            rows.append(jnp.where(inside, jnp.where(lane == o + a, 1.0, 0.0), r))
        more = j + 1 < n
        if more:
            old = x[o + B : o + 2 * B, :]
            c = [across(old, o + k) for k in range(B)]
            following = jnp.where(inside, 0.0, old)
        l = [[None] * B for _ in range(B)]
        scale, v = [], []
        for i in range(B):
            inv = lax.rsqrt(d[i][i])
            scale.append(inv)
            for a in range(i + 1, B):
                l[a][i] = d[a][i] * inv
            for a in range(i + 1, B):
                for b in range(i + 1, a + 1):
                    d[a][b] = d[a][b] - l[a][i] * l[b][i]
            v.append(rows[i] * inv)
            for a in range(i + 1, B):
                rows[a] = rows[a] - l[a][i] * v[i]
            if more:
                scaled = c[i] * inv
                for a in range(i + 1, B):
                    c[a] = c[a] - l[a][i] * scaled
                following = following - scaled * v[i]
        if more:
            x[o + B : o + 2 * B, :] = following
        if j + 2 < n:
            y = [None] * B
            for i in reversed(range(B)):
                t = v[i]
                for a in range(i + 1, B):
                    t = t - l[a][i] * y[a]
                y[i] = t * scale[i]
            for r in range(j + 2, n):
                sl = slice(r * B, (r + 1) * B)
                old = x[sl, :]
                c = [across(old, o + k) for k in range(B)]
                x[sl, :] = jnp.where(inside, 0.0, old) - tree([c[k] * y[k] for k in range(B)])
        for i in range(B):
            x[o + i : o + i + 1, :] = jnp.where(lane < o + B, v[i], 0.0)[0:1, :]


def times_transposed(a, b):
    return lax.dot_general(
        a,
        b,
        (((1,), (1,)), ((), ())),
        precision=lax.Precision.HIGHEST,
        preferred_element_type=jnp.float32,
    )


def finish_kernel(m_ref, own_ref, other_ref, out_ref, a, b):
    core = lax.axis_index("core")
    zero = jnp.where(core == 0, own_ref[...], other_ref[...])
    one = jnp.where(core == 0, other_ref[...], own_ref[...])

    def unpack(packed):
        low = packed[0:64, HALF:K]
        corner = [packed[64:PACKED, 64 * q : 64 * (q + 1)] for q in range(4)]
        top = jnp.concatenate([jnp.concatenate(corner, axis=0), low[:, 0:64].T], axis=1)
        return jnp.concatenate([top, low], axis=0), packed[0:64, 0:HALF]

    a[...], upper = unpack(zero)
    corner, lower = unpack(one)
    below = jnp.concatenate([upper, lower], axis=0)
    chol_inverse(a)
    factor = times_transposed(below, a[...])
    b[...] = corner - times_transposed(factor, factor)
    first = times_transposed(m_ref[:, 0:HALF], a[...])
    rest = m_ref[:, HALF:K] - times_transposed(first, factor)
    chol_inverse(b)
    out_ref[:, 0:HALF] = first
    out_ref[:, HALF:K] = times_transposed(rest, b[...])


def finish(m, own, other):
    vmem = pl.BlockSpec(memory_space=pltpu.VMEM)
    return pl.pallas_call(
        finish_kernel,
        out_shape=blocks(),
        in_specs=[vmem] * 3,
        out_specs=vmem,
        scratch_shapes=[pltpu.VMEM((HALF, HALF), jnp.float32)] * 2,
        compiler_params=pltpu.CompilerParams(vmem_limit_bytes=32 * MIB),
        name="finish",
    )(m, own, other)


FIRST = (2, 1, 3)
DISTANCES = (3, 1, 2)


def ring_pairs(axes, distance):
    pairs = []
    for source in range(128):
        place = {"y": source // 32, "x": source // 8 % 4, "z": source // 2 % 4}
        core = source % 2
        place[axes[core]] = (place[axes[core]] + distance) % 4
        target = ((place["y"] * 4 + place["x"]) * 4 + place["z"]) * 2 + core
        pairs.append((source, target))
    return pairs


def solution(mesh):
    every = ("y", "x", "z", "core")
    fine = Mesh(mesh.devices.reshape(4, 4, 4, 2), every)
    swap = [(0, 1), (1, 0)]

    def along(axes, messages, distances=DISTANCES):
        return [
            lax.ppermute(m, every, ring_pairs(axes, k)) for m, k in zip(messages, distances)
        ]

    def local(embedding, test_matrix):
        place = jnp.stack([lax.axis_index(a) for a in every]).astype(jnp.int32)
        keep, *send, gk, gs = local_products(place, embedding, test_matrix)
        got = [None] * 4
        got[2] = lax.ppermute(send[2], "core", swap)
        gg = lax.ppermute(gs, "core", swap)
        send[1], send[3], send[0], gg = lax.optimization_barrier(
            (send[1], send[3], send[0], gg)
        )
        for k in (1, 3, 0):
            got[k] = lax.ppermute(send[k], "core", swap)
        messages = [message(k, keep, got[k], gk, gg) for k in FIRST]
        arrived = along(("z", "x"), messages, FIRST)
        own, *messages = second(keep, got[0], gk, gg, arrived)
        arrived = along(("y", "z"), messages)
        own, *messages_3 = third(own, messages[0], arrived)
        arrived = along(("x", "y"), messages_3)
        m, g = last(own, messages_3[0], arrived)
        return finish(m, g, lax.ppermute(g, "core", swap))

    return jax.shard_map(
        local,
        mesh=fine,
        in_specs=(P(every, None), P()),
        out_specs=P(every, None),
        check_vma=False,
    )
```

```python
import functools

import jax
import jax.numpy as jnp
from jax import lax
from jax.experimental import pallas as pl
from jax.experimental.pallas import tpu as pltpu
from jax.sharding import Mesh, PartitionSpec as P

K = 256
B = 8
HALF = K // 2
MIB = 1 << 20


def tree(terms):
    while len(terms) > 1:
        terms = [
            terms[i] + terms[i + 1] if i + 1 < len(terms) else terms[i]
            for i in range(0, len(terms), 2)
        ]
    return terms[0]


ROWS_STEP = 512
COLS_STEP = 1024
CHIPS_STEP = COLS_STEP // 64
PACKED = 80
OVER_ROWS = (((0,), (0,)), ((), ()))


def local_kernel(
    steps, place_ref, e_ref, t_ref, keep_ref, s0, s1, s2, s3, gram_keep_ref,
    gram_send_ref, held, t_held, s_ref, gram, parts, sem, t_sem,
):
    i = pl.program_id(0)
    f32 = jnp.float32
    x, z, core = place_ref[1], place_ref[2], place_ref[3]

    def fetch(step):
        r = pl.ds(pl.multiple_of(step * ROWS_STEP, ROWS_STEP), ROWS_STEP)
        return pltpu.make_async_copy(e_ref.at[r], held.at[r], sem.at[step])

    @pl.when(i == 0)
    def _():
        table = pltpu.make_async_copy(t_ref, t_held, t_sem)
        table.start()
        fetch(0).start()
        table.wait()
        fetch(1).start()

        def sketch(step, carry):
            fetch(step).wait()

            @pl.when(step + 2 < steps)
            def _():
                fetch(step + 2).start()

            r = pl.ds(pl.multiple_of(step * ROWS_STEP, ROWS_STEP), ROWS_STEP)
            s = jnp.dot(held[r, :], t_held[...], preferred_element_type=f32)
            hi = s.astype(jnp.bfloat16)
            s_ref[r, 0:K] = hi
            s_ref[r, K : 2 * K] = (s - hi.astype(f32)).astype(jnp.bfloat16)
            return carry

        lax.fori_loop(0, steps, sketch, 0)
        g = lax.dot_general(
            s_ref[:, 0:K], s_ref[...], OVER_ROWS, preferred_element_type=f32
        )
        mixed = g[:, K : 2 * K]
        gram[...] = g[:, 0:K] + (mixed + mixed.T)

        def pack(out, c):
            own = slice(c * HALF, (c + 1) * HALF)
            diagonal = gram[own, own]
            out[0:64, 0:HALF] = gram[HALF + 64 * c : HALF + 64 * (c + 1), 0:HALF]
            out[0:64, HALF:K] = diagonal[64:HALF]
            corner = diagonal[0:64, 0:64]
            out[64:PACKED, :] = jnp.concatenate(
                [corner[16 * q : 16 * (q + 1)] for q in range(4)], axis=1
            )

        @pl.when(core == 0)
        def _():
            pack(gram_keep_ref, 0)
            pack(gram_send_ref, 1)

        @pl.when(core != 0)
        def _():
            pack(gram_keep_ref, 1)
            pack(gram_send_ref, 0)

    @pl.when(i > 0)
    def _():
        c = pl.ds(pl.multiple_of((i - 1) * COLS_STEP, COLS_STEP), COLS_STEP)
        m = lax.dot_general(held[:, c], s_ref[...], OVER_ROWS, preferred_element_type=f32)
        parts[...] = (m[:, 0:K] + m[:, K : 2 * K]).reshape(CHIPS_STEP, 2, 32, K)
        for k, send_ref in enumerate((s0, s1, s2, s3)):
            for o in range(4):
                by_z = 4 * o + ((z + k) & 3)
                by_x = 4 * ((x + k) & 3) + o
                keep_ref[k, 0, o] = parts[jnp.where(core == 0, by_z, by_x), core]
                send_ref[0, o] = parts[jnp.where(core == 0, by_x, by_z), 1 - core]


def blocks(*lead):
    return jax.ShapeDtypeStruct(lead + (32, K), jnp.float32)


def flat(n):
    return jax.ShapeDtypeStruct((32 * n + PACKED, K), jnp.float32)


def local_products(place, e, t):
    rows, d = e.shape
    steps = rows // ROWS_STEP

    def column(i):
        return jnp.maximum(i - 1, 0)

    kept = pl.BlockSpec((4, 1, 4, 32, K), lambda i: (0, column(i), 0, 0, 0))
    sent = pl.BlockSpec((1, 4, 32, K), lambda i: (column(i), 0, 0, 0))
    whole = pl.BlockSpec((PACKED, K), lambda i: (0, 0))
    return pl.pallas_call(
        functools.partial(local_kernel, steps),
        grid_spec=pl.GridSpec(
            grid=(1 + d // COLS_STEP,),
            in_specs=[
                pl.BlockSpec(memory_space=pltpu.SMEM),
                pl.BlockSpec(memory_space=pl.ANY),
                pl.BlockSpec(memory_space=pl.ANY),
            ],
            out_specs=[kept] + [sent] * 4 + [whole] * 2,
            scratch_shapes=[
                pltpu.VMEM((rows, d), jnp.bfloat16),
                pltpu.VMEM((d, K), jnp.bfloat16),
                pltpu.VMEM((rows, 2 * K), jnp.bfloat16),
                pltpu.VMEM((K, K), jnp.float32),
                pltpu.VMEM((CHIPS_STEP, 2, 32, K), jnp.float32),
                pltpu.SemaphoreType.DMA((steps,)),
                pltpu.SemaphoreType.DMA,
            ],
        ),
        out_shape=[blocks(4, 4, 4)] + [blocks(4, 4)] * 4 + [flat(0)] * 2,
        compiler_params=pltpu.CompilerParams(vmem_limit_bytes=46 * MIB),
        cost_estimate=pl.CostEstimate(
            flops=6 * rows * K * d + 8 * rows * K * K,
            bytes_accessed=rows * d * 2 + d * K * 6,
            transcendentals=0,
        ),
        name="local_products",
    )(place, e, pltpu.with_memory_space_constraint(t, pltpu.HBM))


def one_step(kernel, name, out_shape):
    vmem = pl.BlockSpec(memory_space=pltpu.VMEM)

    def call(*args, scratch=()):
        return pl.pallas_call(
            kernel,
            out_shape=out_shape,
            in_specs=[vmem] * len(args),
            out_specs=[vmem] * len(out_shape),
            scratch_shapes=list(scratch),
            compiler_params=pltpu.CompilerParams(vmem_limit_bytes=20 * MIB),
            name=name,
        )(*args)

    return call


def message_kernel(k, keep_ref, got_ref, gk_ref, gg_ref, out_ref):
    out_ref[0:512] = (keep_ref[k] + got_ref[...]).reshape(512, K)
    out_ref[512:] = gk_ref[...] + gg_ref[...]


def message(k, keep, got, gk, gg):
    kernel = functools.partial(message_kernel, k)
    return one_step(kernel, "message", [flat(16)])(keep, got, gk, gg)[0]


def second_kernel(keep_ref, got_ref, gk_ref, gg_ref, a, b, c, own, *refs):
    out, m = refs[:-1], refs[-1]
    core = lax.axis_index("core")
    y, z = lax.axis_index("y"), lax.axis_index("z")
    m[...] = (keep_ref[0] + got_ref[...]) + (a[0:512] + b[0:512] + c[0:512]).reshape(
        4, 4, 32, K
    )
    gram = (gk_ref[...] + gg_ref[...]) + (a[512:] + b[512:] + c[512:])
    for ref, k in zip((own,) + out, (0,) + DISTANCES):
        for i in range(4):
            first = jnp.where(core == 0, (y + k) & 3, i)
            other = jnp.where(core == 0, i, (z + k) & 3)
            ref[32 * i : 32 * (i + 1)] = m[first, other]
    for ref in out:
        ref[128:] = gram


def second(keep, got, gk, gg, arrived):
    outs = [jax.ShapeDtypeStruct((128, K), jnp.float32)] + [flat(4)] * 3
    scratch = [pltpu.VMEM((4, 4, 32, K), jnp.float32)]
    return one_step(second_kernel, "second", outs)(
        keep, got, gk, gg, *arrived, scratch=scratch
    )


def third_kernel(own_ref, sent, a, b, c, own, *refs):
    out, m = refs[:-1], refs[-1]
    m[...] = (own_ref[...] + (a[0:128] + b[0:128] + c[0:128])).reshape(4, 32, K)
    gram = sent[128:] + (a[128:] + b[128:] + c[128:])
    at = jnp.where(lax.axis_index("core") == 0, lax.axis_index("x"), lax.axis_index("y"))
    own[...] = m[at]
    for ref, k in zip(out, DISTANCES):
        ref[0:32] = m[(at + k) & 3]
        ref[32:] = gram


def third(own, sent, arrived):
    outs = [blocks()] + [flat(1)] * 3
    scratch = [pltpu.VMEM((4, 32, K), jnp.float32)]
    return one_step(third_kernel, "third", outs)(own, sent, *arrived, scratch=scratch)


def last_kernel(own_ref, sent, a, b, c, m_ref, g_ref):
    m_ref[...] = own_ref[...] + (a[0:32] + b[0:32] + c[0:32])
    g_ref[...] = sent[32:] + (a[32:] + b[32:] + c[32:])


def last(own, sent, arrived):
    return one_step(last_kernel, "last", [blocks(), flat(0)])(own, sent, *arrived)


def across(v, lane):
    return jnp.take_along_axis(v, jnp.full(v.shape, lane, jnp.int32), axis=1)


def chol_inverse(x):
    lane = lax.broadcasted_iota(jnp.int32, (B, HALF), 1)
    n = HALF // B
    panel = x[0:B, :]
    for j in range(n):
        o = j * B
        inside = (lane >= o) & (lane < o + B)
        cols = [across(panel, o + b) for b in range(B)]
        d = [
            [jnp.broadcast_to(cols[b][a : a + 1, :], (B, HALF)) for b in range(a + 1)]
            for a in range(B)
        ]
        rows = []
        for a in range(B):
            r = jnp.broadcast_to(x[o + a : o + a + 1, :], (B, HALF))
            rows.append(jnp.where(inside, jnp.where(lane == o + a, 1.0, 0.0), r))
        more = j + 1 < n
        if more:
            old = x[o + B : o + 2 * B, :]
            c = [across(old, o + k) for k in range(B)]
            following = jnp.where(inside, 0.0, old)
        l = [[None] * B for _ in range(B)]
        scale, v = [], []
        for i in range(B):
            inv = lax.rsqrt(d[i][i])
            scale.append(inv)
            for a in range(i + 1, B):
                l[a][i] = d[a][i] * inv
            for a in range(i + 1, B):
                for b in range(i + 1, a + 1):
                    d[a][b] = d[a][b] - l[a][i] * l[b][i]
            v.append(rows[i] * inv)
            for a in range(i + 1, B):
                rows[a] = rows[a] - l[a][i] * v[i]
            if more:
                scaled = c[i] * inv
                for a in range(i + 1, B):
                    c[a] = c[a] - l[a][i] * scaled
                following = following - scaled * v[i]
        if more:
            x[o + B : o + 2 * B, :] = following
            panel = following
        if j + 2 < n:
            y = [None] * B
            for i in reversed(range(B)):
                t = v[i]
                for a in range(i + 1, B):
                    t = t - l[a][i] * y[a]
                y[i] = t * scale[i]
            for r in range(j + 2, n):
                sl = slice(r * B, (r + 1) * B)
                old = x[sl, :]
                c = [across(old, o + k) for k in range(B)]
                x[sl, :] = jnp.where(inside, 0.0, old) - tree([c[k] * y[k] for k in range(B)])
        for i in range(B):
            x[o + i : o + i + 1, :] = jnp.where(lane < o + B, v[i], 0.0)[0:1, :]


def times_transposed(a, b):
    return lax.dot_general(
        a,
        b,
        (((1,), (1,)), ((), ())),
        precision=lax.Precision.HIGHEST,
        preferred_element_type=jnp.float32,
    )


def finish_kernel(m_ref, own_ref, other_ref, out_ref, a, b):
    core = lax.axis_index("core")
    zero = jnp.where(core == 0, own_ref[...], other_ref[...])
    one = jnp.where(core == 0, other_ref[...], own_ref[...])

    def unpack(packed):
        low = packed[0:64, HALF:K]
        corner = [packed[64:PACKED, 64 * q : 64 * (q + 1)] for q in range(4)]
        top = jnp.concatenate([jnp.concatenate(corner, axis=0), low[:, 0:64].T], axis=1)
        return jnp.concatenate([top, low], axis=0), packed[0:64, 0:HALF]

    a[...], upper = unpack(zero)
    corner, lower = unpack(one)
    below = jnp.concatenate([upper, lower], axis=0)
    chol_inverse(a)
    factor = times_transposed(below, a[...])
    b[...] = corner - times_transposed(factor, factor)
    first = times_transposed(m_ref[:, 0:HALF], a[...])
    rest = m_ref[:, HALF:K] - times_transposed(first, factor)
    chol_inverse(b)
    out_ref[:, 0:HALF] = first
    out_ref[:, HALF:K] = times_transposed(rest, b[...])


def finish(m, own, other):
    vmem = pl.BlockSpec(memory_space=pltpu.VMEM)
    return pl.pallas_call(
        finish_kernel,
        out_shape=blocks(),
        in_specs=[vmem] * 3,
        out_specs=vmem,
        scratch_shapes=[pltpu.VMEM((HALF, HALF), jnp.float32)] * 2,
        compiler_params=pltpu.CompilerParams(vmem_limit_bytes=32 * MIB),
        name="finish",
    )(m, own, other)


FIRST = (2, 1, 3)
DISTANCES = (3, 1, 2)


def ring_pairs(axes, distance):
    pairs = []
    for source in range(128):
        place = {"y": source // 32, "x": source // 8 % 4, "z": source // 2 % 4}
        core = source % 2
        place[axes[core]] = (place[axes[core]] + distance) % 4
        target = ((place["y"] * 4 + place["x"]) * 4 + place["z"]) * 2 + core
        pairs.append((source, target))
    return pairs


def solution(mesh):
    every = ("y", "x", "z", "core")
    fine = Mesh(mesh.devices.reshape(4, 4, 4, 2), every)
    swap = [(0, 1), (1, 0)]

    def along(axes, messages, distances=DISTANCES):
        return [
            lax.ppermute(m, every, ring_pairs(axes, k)) for m, k in zip(messages, distances)
        ]

    def local(embedding, test_matrix):
        place = jnp.stack([lax.axis_index(a) for a in every]).astype(jnp.int32)
        keep, *send, gk, gs = local_products(place, embedding, test_matrix)
        got = [None] * 4
        got[2] = lax.ppermute(send[2], "core", swap)
        gg = lax.ppermute(gs, "core", swap)
        send[1], send[3], send[0], gg = lax.optimization_barrier(
            (send[1], send[3], send[0], gg)
        )
        for k in (1, 3, 0):
            got[k] = lax.ppermute(send[k], "core", swap)
        messages = [message(k, keep, got[k], gk, gg) for k in FIRST]
        arrived = along(("z", "x"), messages, FIRST)
        own, *messages = second(keep, got[0], gk, gg, arrived)
        arrived = along(("y", "z"), messages)
        own, *messages_3 = third(own, messages[0], arrived)
        arrived = along(("x", "y"), messages_3)
        m, g = last(own, messages_3[0], arrived)
        return finish(m, g, lax.ppermute(g, "core", swap))

    return jax.shard_map(
        local,
        mesh=fine,
        in_specs=(P(every, None), P()),
        out_specs=P(every, None),
        check_vma=False,
    )
```
